128 devices in a mesh: gy: 8 (over z_lo, y), gx: 16 (over z_hi, x, core).
Axes of the slice: x: 4, y: 4, z: 4 (z_hi: 2, z_lo: 2; z = z_hi * 2 + z_lo), core: 2. Of those that a mesh axis runs over, the one named last changes fastest.
Arguments:
- occupancy: int32 [2, 40, 512, 512], P(None, None, 'gy', 'gx'), may hold values 0 or 1
- counts: int32 [2, 512, 512], P(None, 'gy', 'gx'), may hold values from 0 to 64
- level_embed: bfloat16 [40, 256], replicated, may hold values from -1.796875 to 1.796875
- count_weight: float32 [256], replicated, may hold values from -3 to 3
- norm_gains: float32 [2, 256], replicated, may hold values from 0.1 to 1.9
- row_qkv: bfloat16 [256, 768], replicated, may hold values from -2 to 2
- row_out: bfloat16 [256, 256], replicated, may hold values from -0.375 to 0.375
- col_qkv: bfloat16 [256, 768], replicated, may hold values from -2 to 2
- col_out: bfloat16 [256, 256], replicated, may hold values from -0.375 to 0.375
- depth_kernel: float32 [3, 3, 256], replicated, may hold values from -2 to 2
- point_weight: bfloat16 [256, 256], replicated, may hold values from -0.375 to 0.375
Outputs:
- bev_out: bfloat16 [2, 512, 512, 256], P(None, 'gy', 'gx')
The draws below stay inside these ranges and needn't reach their ends.
All inputs are finite; a program needn't handle non-finite values. No bound on the sum of `occupancy` on one device may be relied on, other than what follows from the above.
Results may differ from the reference program's by a relative error of at most 0.015.
The reference program's roundings to bfloat16 on the way count: a program that leaves them out, or rounds other values in their place, can miss the bound.
Values may be sent and summed in bfloat16 or wider, within the bound.
A program may use at most 128 MiB of HBM per device.

```python
import jax
import jax.numpy as jnp
from jax import lax

C = 256
HEADS = 8
LEVELS = 40
BATCH = 2
H = 512
W = 512


def projection_draw(seed_key):
    subkeys = jax.random.split(seed_key, 1)
    whole = jnp.clip(jax.random.normal(subkeys[0], (C, 3 * C), jnp.float32), -6.0, 6.0) * C ** (-0.5)
    return whole.astype(jnp.bfloat16)


def draw_row_qkv(key, part):
    return projection_draw(jax.random.fold_in(key, 11))


def draw_col_qkv(key, part):
    return projection_draw(jax.random.fold_in(key, 23))


def plant(array, key, smallest, largest):
    spot = [jax.random.randint(jax.random.fold_in(key, axis), (), 0, length) for axis, length in enumerate(array.shape)]
    main_axis = array.shape.index(max(array.shape))
    next_to = spot[:main_axis] + [(spot[main_axis] + 1) % array.shape[main_axis]] + spot[main_axis + 1:]
    return array.at[tuple(spot)].set(smallest).at[tuple(next_to)].set(largest)


def normal_values(rng, shape, spread, bound, dtype=jnp.bfloat16):
    return jnp.clip(spread * jax.random.normal(rng, shape, jnp.float32), -bound, bound).astype(dtype)


def setup_inputs(seed: int = 0) -> dict:
    arg_keys = jax.random.split(jax.random.key(seed), 12)
    occupancy = plant((jax.random.randint(arg_keys[0], (BATCH, LEVELS, H, W), 0, 2) < 1).astype(jnp.int32), jax.random.fold_in(arg_keys[0], 1), 0, 1)
    counts = plant(jax.random.randint(arg_keys[1], (BATCH, H, W), 0, 65), jax.random.fold_in(arg_keys[1], 1), 0, 64).astype(jnp.int32)
    level_embed = normal_values(arg_keys[2], (LEVELS, C), 0.3, 1.796875)
    count_weight = normal_values(arg_keys[3], (C,), 0.5, 3.0, jnp.float32)
    norm_gains = jnp.clip(1.0 + 0.18 * jax.random.normal(arg_keys[4], (2, C), jnp.float32), 0.1, 1.9)
    row_qkv = draw_row_qkv(jax.random.fold_in(arg_keys[11], 71), 0)
    row_out = normal_values(arg_keys[6], (C, C), C ** -0.5, 0.375)
    col_qkv = draw_col_qkv(jax.random.fold_in(arg_keys[11], 71), 0)
    col_out = normal_values(arg_keys[8], (C, C), C ** -0.5, 0.375)
    depth_kernel = normal_values(arg_keys[9], (3, 3, C), 0.35, 2.0, jnp.float32)
    point_weight = normal_values(arg_keys[10], (C, C), C ** -0.5, 0.375)
    return {"occupancy": occupancy, "counts": counts, "level_embed": level_embed, "count_weight": count_weight, "norm_gains": norm_gains, "row_qkv": row_qkv, "row_out": row_out, "col_qkv": col_qkv, "col_out": col_out, "depth_kernel": depth_kernel, "point_weight": point_weight}


def layer_norm(source, gain_vec):
    wide_x = source.astype(jnp.float32)
    row_mean = lax.optimization_barrier(jnp.mean(wide_x, -1, keepdims=True))
    centred = wide_x - row_mean
    variance = lax.optimization_barrier(jnp.mean(centred * centred, -1, keepdims=True))
    return (centred * lax.rsqrt(variance + 1e-05) * gain_vec).astype(jnp.bfloat16)

def attend_line(packed):
    channels = packed.shape[-1] // 3
    length = packed.shape[0]
    head_dim = channels // HEADS
    queries = packed[:, :channels].astype(jnp.float32).reshape(length, HEADS, head_dim)
    keyset = packed[:, channels:2 * channels].astype(jnp.float32).reshape(length, HEADS, head_dim)
    values = packed[:, 2 * channels:].astype(jnp.float32).reshape(length, HEADS, head_dim)
    scores = jnp.einsum('qhd,khd->hqk', queries, keyset) * head_dim ** (-0.5)
    row_max = lax.optimization_barrier(jnp.max(scores, -1, keepdims=True))
    weights = jnp.exp(scores - row_max)
    probs = (weights / lax.optimization_barrier(jnp.sum(weights, -1, keepdims=True))).astype(jnp.bfloat16)
    attended = jnp.einsum('hqk,khd->qhd', probs.astype(jnp.float32), values)
    return attended.reshape(length, channels).astype(jnp.bfloat16)

def axial_rows(source, gain_vec, w_qkv, w_out):
    normed = layer_norm(source, gain_vec)
    packed = jnp.dot(normed, w_qkv, preferred_element_type=jnp.float32).astype(jnp.bfloat16)
    dims_now = packed.shape
    attended = lax.map(attend_line, packed.reshape(-1, dims_now[2], dims_now[3]))
    attended = attended.reshape(dims_now[0], dims_now[1], dims_now[2], -1)
    return (source.astype(jnp.float32) + jnp.dot(attended, w_out, preferred_element_type=jnp.float32)).astype(jnp.bfloat16)

def reference(occupancy, counts, level_embed, count_weight, norm_gains, row_qkv, row_out, col_qkv, col_out, depth_kernel, point_weight):
    base = jnp.einsum('blhw,lc->bhwc', occupancy.astype(jnp.float32), level_embed.astype(jnp.float32))
    count_term = jnp.log1p(counts.astype(jnp.float32))[..., None] * count_weight
    pillars = (base + count_term).astype(jnp.bfloat16)
    rows_done = axial_rows(pillars, norm_gains[0], row_qkv, row_out)
    turned = rows_done.transpose(0, 2, 1, 3)
    cols_done = axial_rows(turned, norm_gains[1], col_qkv, col_out).transpose(0, 2, 1, 3)
    padded = jnp.pad(cols_done, ((0, 0), (1, 1), (1, 1), (0, 0)))
    depth_sum = jnp.zeros(cols_done.shape, jnp.float32)
    for row_off in range(3):
        for col_off in range(3):
            depth_sum = depth_sum + padded[:, row_off:row_off + H, col_off:col_off + W, :].astype(jnp.float32) * depth_kernel[row_off, col_off]
    activated = jax.nn.silu(depth_sum).astype(jnp.bfloat16)
    return (cols_done.astype(jnp.float32) + jnp.dot(activated, point_weight, preferred_element_type=jnp.float32)).astype(jnp.bfloat16)
```

```python
import functools

import jax
import jax.numpy as jnp
from jax import lax
from jax.experimental import pallas as pl
from jax.experimental.pallas import tpu as pltpu
from jax.sharding import PartitionSpec as P

HEADS = 8
BF = jnp.bfloat16
F32 = jnp.float32
LOG2E = 1.4426950408889634
MESH = pl.DeviceIdType.MESH
DEPTH = 48


def dot(a, b):
    return jnp.dot(a, b, preferred_element_type=F32)


def section(x, gain, wqkv_ref, wout_ref):
    length, ch = x.shape
    half_ch = ch // 2
    head_dim = ch // HEADS
    cen = x - jnp.mean(x, -1, keepdims=True)
    var = jnp.mean(cen * cen, -1, keepdims=True)
    normed = (cen * lax.rsqrt(var + 1e-5) * gain).astype(BF)
    q = (dot(normed, wqkv_ref[:, :ch]) * (LOG2E * head_dim ** -0.5)).astype(BF)
    k = dot(normed, wqkv_ref[:, ch : 2 * ch]).astype(BF)
    v = dot(normed, wqkv_ref[:, 2 * ch :]).astype(BF)
    ones = jnp.ones((length, half_ch), BF)
    lane = lax.broadcasted_iota(jnp.int32, (1, ch), 1) // head_dim
    halves = []
    for half in range(2):
        num = den = None
        vals = jnp.concatenate([v[:, half * half_ch : (half + 1) * half_ch], ones], 1)
        for head in range(half * HEADS // 2, (half + 1) * HEADS // 2):
            qm = jnp.where(lane == head, q, BF(0))
            s = lax.dot_general(qm, k, (((1,), (1,)), ((), ())), preferred_element_type=F32)
            e = jnp.exp2(s - jnp.max(s, -1, keepdims=True)).astype(BF)
            r = dot(e, vals)
            if num is None:
                num, den = r[:, :half_ch], r[:, half_ch:]
            else:
                mine = lane[:, half * half_ch : (half + 1) * half_ch] == head
                num = jnp.where(mine, r[:, :half_ch], num)
                den = jnp.where(mine, r[:, half_ch:], den)
        halves.append((num / den).astype(BF))
    return x + dot(jnp.concatenate(halves, 1), wout_ref[...])


class Plan:
    def __init__(self, ny, nx, height, width):
        self.ny, self.nx = ny, nx
        self.height, self.width = height, width
        self.th, self.tw = height // ny, width // nx
        self.rows = 2 * self.th // nx
        self.cols = 2 * self.tw // ny
        self.groups = width // self.cols
        self.per_tile = ny // 2

    def me(self):
        gy, gx = lax.axis_index("gy"), lax.axis_index("gx")
        return gy, gx, lax.rem(gx + gy, 2)

    def owner(self, group, sample):
        gx = group // self.per_tile
        gy = 2 * lax.rem(group, self.per_tile) + lax.rem(sample + gx, 2)
        return (gy, gx)


def row_kernel(pn, feat_ref, emb_ref, g_ref, wqkv_ref, wout_ref, out_ref, x_s, s_s, send_sem, recv_sem, own_sem):
    gy, gx, sample = pn.me()
    ch = emb_ref.shape[1]
    group = gx * pn.per_tile + gy // 2
    row_group = gy * (pn.nx // 2) + gx // 2
    barrier = pltpu.get_barrier_semaphore()

    def greet(t, carry):
        other = pn.owner(lax.rem(group + t, pn.groups), sample)
        pl.semaphore_signal(barrier, inc=1, device_id=other, device_id_type=MESH)
        return carry

    lax.fori_loop(1, pn.groups, greet, 0)

    def pillars(src, carry):
        p = lax.dot_general(feat_ref[src], emb_ref[...], (((0,), (0,)), ((), ())), preferred_element_type=F32)
        x_s[:, pl.ds(pl.multiple_of(src * pn.tw, pn.tw), pn.tw), :] = p.astype(BF).reshape(pn.rows, pn.tw, ch)
        return carry

    lax.fori_loop(0, pn.nx, pillars, 0)
    pl.semaphore_wait(barrier, pn.groups - 1)

    def pair(p, carry):
        done = [
            section(x_s[2 * p + i].astype(F32), g_ref[...], wqkv_ref, wout_ref).reshape(pn.groups, pn.cols, ch)
            for i in range(2)
        ]
        s_s[p] = jnp.concatenate(done, 1).astype(BF)

        def send(t, c):
            to = lax.rem(group + t, pn.groups)
            pltpu.make_async_remote_copy(
                src_ref=s_s.at[p, to],
                dst_ref=out_ref.at[row_group, p],
                send_sem=send_sem,
                recv_sem=recv_sem,
                device_id=pn.owner(to, sample),
                device_id_type=MESH,
            ).start()
            return c

        lax.fori_loop(1, pn.groups, send, 0)
        return carry

    lax.fori_loop(0, pn.rows // 2, pair, 0)
    own = pltpu.make_async_copy(s_s.at[:, group], out_ref.at[row_group], own_sem)
    own.start()
    own.wait()
    arrived = out_ref.at[pl.ds(0, pn.groups - 1)]
    pltpu.make_async_copy(arrived, arrived, send_sem).wait()
    pltpu.make_async_copy(arrived, arrived, recv_sem).wait()


def row_phase(pn, feat, emb, gain, wqkv, wout):
    ch = emb.shape[1]
    vmem = pl.BlockSpec(memory_space=pltpu.VMEM)
    pairs = pn.rows // 2
    return pl.pallas_call(
        functools.partial(row_kernel, pn),
        out_shape=jax.ShapeDtypeStruct((pn.groups, pairs, 2 * pn.cols, ch), BF),
        in_specs=[vmem] * 5,
        out_specs=pl.BlockSpec(memory_space=pl.ANY),
        scratch_shapes=[
            pltpu.VMEM((pn.rows, pn.width, ch), BF),
            pltpu.VMEM((pairs, pn.groups, 2 * pn.cols, ch), BF),
            pltpu.SemaphoreType.DMA,
            pltpu.SemaphoreType.DMA,
            pltpu.SemaphoreType.DMA,
        ],
        compiler_params=pltpu.CompilerParams(
            collective_id=0, has_side_effects=True, vmem_limit_bytes=56 * 2**20
        ),
        name="row_phase",
    )(feat, emb, gain, wqkv, wout)


def col_kernel(
    pn, x_ref, g_ref, wqkv_ref, wout_ref, dk_ref, pw_ref, out_ref, cd_s, o_s, hsend, hrecv, send_sem, recv_sem, own_sem
):
    gy, gx, sample = pn.me()
    group = gx * pn.per_tile + gy // 2
    first = sample * pn.tw + (gy // 2) * pn.cols
    has_left, has_right = group > 0, group < pn.groups - 1
    left = pn.owner(jnp.maximum(group - 1, 0), sample)
    right = pn.owner(jnp.minimum(group + 1, pn.groups - 1), sample)
    last = pn.cols - 1
    barrier = pltpu.get_barrier_semaphore()

    def greet(t, carry):
        pl.semaphore_signal(
            barrier, inc=1, device_id=(lax.rem(gy + t, pn.ny), gx), device_id_type=MESH
        )
        return carry

    lax.fori_loop(1, pn.ny, greet, 0)

    @pl.when(has_left)
    def _():
        pl.semaphore_signal(barrier, inc=1, device_id=left, device_id_type=MESH)

    @pl.when(has_right)
    def _():
        pl.semaphore_signal(barrier, inc=1, device_id=right, device_id_type=MESH)

    zeros = jnp.zeros(cd_s.shape[1:], BF)

    @pl.when(jnp.logical_not(has_left))
    def _():
        cd_s[0] = zeros

    @pl.when(jnp.logical_not(has_right))
    def _():
        cd_s[pn.cols + 1] = zeros

    to_left = pltpu.make_async_remote_copy(
        src_ref=cd_s.at[1],
        dst_ref=cd_s.at[pn.cols + 1],
        send_sem=hsend.at[0],
        recv_sem=hrecv.at[0],
        device_id=left,
        device_id_type=MESH,
    )
    to_right = pltpu.make_async_remote_copy(
        src_ref=cd_s.at[pn.cols],
        dst_ref=cd_s.at[0],
        send_sem=hsend.at[1],
        recv_sem=hrecv.at[1],
        device_id=right,
        device_id_type=MESH,
    )
    row = lax.broadcasted_iota(jnp.int32, (pn.height, 1), 0)

    def conv(c):
        near = [cd_s[c + i].astype(F32) for i in range(3)]
        taps = [sum(near[e] * dk_ref[a, e, :][None] for e in range(3)) for a in range(3)]
        above = jnp.where(row == 0, 0.0, pltpu.roll(taps[0], 1, 0))
        below = jnp.where(row == pn.height - 1, 0.0, pltpu.roll(taps[2], pn.height - 1, 0))
        depth = above + taps[1] + below
        act = (depth / (1.0 + jnp.exp(-depth))).astype(BF)
        o_s[c] = (near[1] + dot(act, pw_ref[...])).astype(BF)

        def send(t, carry):
            to = lax.rem(gy + t, pn.ny)
            pltpu.make_async_remote_copy(
                src_ref=o_s.at[c, pl.ds(pl.multiple_of(to * pn.th, pn.th), pn.th)],
                dst_ref=out_ref.at[first + c],
                send_sem=send_sem,
                recv_sem=recv_sem,
                device_id=(to, gx),
                device_id_type=MESH,
            ).start()
            return carry

        lax.fori_loop(1, pn.ny, send, 0)

    def line(t, carry):
        c = jnp.where(t == 0, 0, jnp.where(t == 1, last, t - 1))
        cd_s[c + 1] = section(x_ref[c].astype(F32), g_ref[...], wqkv_ref, wout_ref).astype(BF)

        @pl.when(jnp.logical_and(t == 0, has_left))
        def _():
            to_left.start()

        @pl.when(jnp.logical_and(t == 1, has_right))
        def _():
            to_right.start()

        @pl.when(t >= 2)
        def _():
            @pl.when(jnp.logical_and(t == 2, has_left))
            def _():
                to_right.wait_recv()

            conv(t - 2)

        return carry

    pl.semaphore_wait(barrier, pn.ny - 1 + has_left.astype(jnp.int32) + has_right.astype(jnp.int32))
    lax.fori_loop(0, pn.cols, line, 0)

    def tail(c, carry):
        @pl.when(jnp.logical_and(c == last, has_right))
        def _():
            to_left.wait_recv()

        conv(c)
        return carry

    lax.fori_loop(pn.cols - 2, pn.cols, tail, 0)

    own = pltpu.make_async_copy(
        o_s.at[:, pl.ds(pl.multiple_of(gy * pn.th, pn.th), pn.th)], out_ref.at[pl.ds(first, pn.cols)], own_sem
    )
    own.start()
    own.wait()

    @pl.when(has_left)
    def _():
        to_left.wait_send()

    @pl.when(has_right)
    def _():
        to_right.wait_send()

    arrived = out_ref.at[pl.ds(0, (pn.ny - 1) * pn.cols)]
    pltpu.make_async_copy(arrived, arrived, send_sem).wait()
    pltpu.make_async_copy(arrived, arrived, recv_sem).wait()


def col_phase(pn, cols, gain, wqkv, wout, dk, pw):
    ch = cols.shape[-1]
    vmem = pl.BlockSpec(memory_space=pltpu.VMEM)
    return pl.pallas_call(
        functools.partial(col_kernel, pn),
        out_shape=jax.ShapeDtypeStruct((2 * pn.tw, pn.th, ch), BF),
        in_specs=[vmem] * 6,
        out_specs=pl.BlockSpec(memory_space=pl.ANY),
        scratch_shapes=[
            pltpu.VMEM((pn.cols + 2, pn.height, ch), BF),
            pltpu.VMEM((pn.cols, pn.height, ch), BF),
            pltpu.SemaphoreType.DMA((2,)),
            pltpu.SemaphoreType.DMA((2,)),
            pltpu.SemaphoreType.DMA,
            pltpu.SemaphoreType.DMA,
            pltpu.SemaphoreType.DMA,
        ],
        compiler_params=pltpu.CompilerParams(
            collective_id=1, has_side_effects=True, vmem_limit_bytes=56 * 2**20
        ),
        name="col_phase",
    )(cols, gain, wqkv, wout, dk, pw)


def split3(x):
    a = lax.reduce_precision(x, 8, 7)
    b = lax.reduce_precision(x - a, 8, 7)
    c = lax.reduce_precision(x - a - b, 8, 7)
    return a, b, c


def per_device(
    occupancy,
    counts,
    level_embed,
    count_weight,
    norm_gains,
    row_qkv,
    row_out,
    col_qkv,
    col_out,
    depth_kernel,
    point_weight,
):
    ny, nx = lax.axis_size("gy"), lax.axis_size("gx")
    th, tw = counts.shape[1:]
    levels, ch = level_embed.shape
    pn = Plan(ny, nx, th * ny, tw * nx)
    gy = lax.axis_index("gy")

    l1, l2, l3 = split3(jnp.log1p(counts.astype(F32)))
    w1, w2, w3 = split3(count_weight)
    zero = jnp.zeros_like(l1)
    feat = jnp.concatenate(
        [occupancy.astype(BF), jnp.stack([l1, l1, l1, l2, l2, l3] + [zero] * (DEPTH - levels - 6), 1).astype(BF)], 1
    )
    emb = jnp.concatenate(
        [
            level_embed,
            jnp.stack([w1, w2, w3, w1, w2, w1]).astype(BF),
            jnp.zeros((DEPTH - levels - 6, ch), BF),
        ]
    )
    feat = jnp.where(lax.rem(gy, 2) == 1, feat[::-1], feat)
    feat = feat.reshape(2, DEPTH, nx // 2, pn.rows, tw).transpose(2, 0, 1, 3, 4).reshape(nx, DEPTH, pn.rows * tw)
    feat = lax.all_to_all(feat, "gx", split_axis=0, concat_axis=0, tiled=True)

    got = row_phase(pn, feat, emb, norm_gains[:1], row_qkv, row_out)
    cols = got.reshape(pn.height, pn.cols, ch).transpose(1, 0, 2)
    out = col_phase(pn, cols, norm_gains[1:], col_qkv, col_out, depth_kernel, point_weight)
    return out.reshape(2, tw, th, ch).transpose(0, 2, 1, 3)


def solution(mesh):
    in_specs = (P(None, None, "gy", "gx"), P(None, "gy", "gx")) + (P(),) * 9
    out_specs = P(None, "gy", "gx", None)
    return jax.shard_map(
        per_device, mesh=mesh, in_specs=in_specs, out_specs=out_specs, check_vma=False
    )
```

```python
import functools

import jax
import jax.numpy as jnp
from jax import lax
from jax.experimental import pallas as pl
from jax.experimental.pallas import tpu as pltpu
from jax.sharding import PartitionSpec as P

HEADS = 8
BF = jnp.bfloat16
F32 = jnp.float32
LOG2E = 1.4426950408889634
MESH = pl.DeviceIdType.MESH
DEPTH = 48
LANES = 128


def dot(a, b):
    return jnp.dot(a, b, preferred_element_type=F32)


def section(x, gain, wqkv_ref, wout_ref):
    length, ch = x.shape
    half_ch = ch // 2
    head_dim = ch // HEADS
    cen = x - jnp.mean(x, -1, keepdims=True)
    var = jnp.mean(cen * cen, -1, keepdims=True)
    normed = (cen * lax.rsqrt(var + 1e-5) * gain).astype(BF)
    q = (dot(normed, wqkv_ref[:, :ch]) * (LOG2E * head_dim ** -0.5)).astype(BF)
    k = dot(normed, wqkv_ref[:, ch : 2 * ch]).astype(BF)
    v = dot(normed, wqkv_ref[:, 2 * ch :]).astype(BF)
    ones = jnp.ones((length, half_ch), BF)
    lane = lax.broadcasted_iota(jnp.int32, (1, ch), 1) // head_dim
    halves = []
    for half in range(2):
        num = den = None
        vals = jnp.concatenate([v[:, half * half_ch : (half + 1) * half_ch], ones], 1)
        for head in range(half * HEADS // 2, (half + 1) * HEADS // 2):
            qm = jnp.where(lane == head, q, BF(0))
            s = lax.dot_general(qm, k, (((1,), (1,)), ((), ())), preferred_element_type=F32)
            e = jnp.exp2(s - jnp.max(s, -1, keepdims=True)).astype(BF)
            r = dot(e, vals)
            if num is None:
                num, den = r[:, :half_ch], r[:, half_ch:]
            else:
                mine = lane[:, half * half_ch : (half + 1) * half_ch] == head
                num = jnp.where(mine, r[:, :half_ch], num)
                den = jnp.where(mine, r[:, half_ch:], den)
        halves.append((num / den).astype(BF))
    return x + dot(jnp.concatenate(halves, 1), wout_ref[...])


def split3(x):
    a = x.astype(BF).astype(F32)
    b = (x - a).astype(BF).astype(F32)
    return a, b, x - a - b


class Plan:
    def __init__(self, ny, nx, height, width):
        self.ny, self.nx = ny, nx
        self.n = ny * nx
        self.height, self.width = height, width
        self.th, self.tw = height // ny, width // nx
        self.rows = height // self.n
        self.cols = width // self.n
        self.per_group = LANES // self.tw
        self.pairs = DEPTH // self.per_group // 2

    def snake(self, q):
        return jnp.where(q < self.ny // 2, q, 3 * self.ny // 2 - 1 - q)

    def owner(self, group):
        m = lax.rem(group, 2 * self.ny)
        return (self.snake(m // 2), 2 * (group // (2 * self.ny)) + lax.rem(m, 2))


def kernel(
    pn,
    occ_ref, cnt_ref, emb_ref, cw_ref, g_ref, rqkv_ref, rout_ref, cqkv_ref, cout_ref, dk_ref, pw_ref,
    out_ref,
    snd_s, got_s, lhs_s, ee_s, x_s, s_s, r_s, xr_s, cd_s, o_s,
    occ_sems, row_send, row_recv, hsend, hrecv, out_sems,
):
    ny, nx, n = pn.ny, pn.nx, pn.n
    th, tw, rows, cols = pn.th, pn.tw, pn.rows, pn.cols
    ch = emb_ref.shape[1]
    levels = emb_ref.shape[0]
    gy, gx = lax.axis_index("gy"), lax.axis_index("gx")
    core = lax.rem(gx, 2)
    m = 2 * pn.snake(gy) + core
    group = (gx // 2) * (2 * ny) + m
    row_group = gy * nx + gx
    tile_x = 2 * (gx // 2) + m // ny
    first = lax.rem(m, ny) * cols
    has_left, has_right = group > 0, group < n - 1
    left = pn.owner(jnp.maximum(group - 1, 0))
    right = pn.owner(jnp.minimum(group + 1, n - 1))
    barrier = pltpu.get_barrier_semaphore()

    def greet(t, carry):
        pl.semaphore_signal(
            barrier, inc=1, device_id=pn.owner(lax.rem(group + t, n)), device_id_type=MESH
        )
        return carry

    lax.fori_loop(1, n, greet, 0)

    def lined_up(b):
        logs = split3(jnp.log1p(cnt_ref[b].astype(F32)))
        terms = [logs[i] for i in (0, 0, 0, 1, 1, 2)]
        return jnp.concatenate(
            [occ_ref[b].astype(F32).reshape(levels * tw, th)]
            + terms
            + [jnp.zeros(((DEPTH - levels - len(terms)) * tw, th), F32)],
            0,
        )

    turned = jnp.concatenate([lined_up(0), lined_up(1)], 1).T
    t0 = turned[:th].reshape(th // 8, 8, DEPTH * tw)
    t1 = turned[th:].reshape(th // 8, 8, DEPTH * tw)
    sub = lax.broadcasted_iota(jnp.int32, (1, 8, 1), 1) < 4
    both = (jnp.where(sub, t0, pltpu.roll(t1, 4, 1)), jnp.where(sub, pltpu.roll(t0, 4, 1), t1))
    for t in range(th // 8):
        for i in range(2):
            for p in range(pn.pairs):
                part = both[i][t][:, 2 * p * LANES : 2 * (p + 1) * LANES]
                snd_s[2 * t + i, p] = jnp.concatenate([part[:, :LANES], part[:, LANES:]], 0).astype(BF)

    pl.semaphore_wait(barrier, n - 1)

    def send_occ(t, carry):
        to = lax.rem(gx + t, nx)
        pltpu.make_async_remote_copy(
            src_ref=snd_s.at[to],
            dst_ref=got_s.at[gx],
            send_sem=occ_sems.at[0],
            recv_sem=occ_sems.at[1],
            device_id=(gy, to),
            device_id_type=MESH,
        ).start()
        return carry

    lax.fori_loop(1, nx, send_occ, 0)
    got_s[gx] = snd_s[gx]

    w1, w2, w3 = split3(cw_ref[...])
    table = [emb_ref[i : i + 1, :].astype(F32) for i in range(levels)] + [w1, w2, w3, w1, w2, w1]
    zero = jnp.zeros((8, ch), F32)
    for i in range(pn.per_group):
        for j in range(LANES // 8):
            at = j * pn.per_group + i
            r0 = i * LANES + j * 8
            ee_s[r0 : r0 + 8, :] = jnp.broadcast_to(table[at], (8, ch)) if at < len(table) else zero

    for s in range(2):
        arrived = got_s.at[pl.ds(0, nx - 1)]
        pltpu.make_async_copy(arrived, arrived, occ_sems.at[s]).wait()

    def unpack(src, carry):
        rows_in = got_s[src].reshape(pn.pairs * 16, LANES).astype(F32)
        pad = jnp.zeros((LANES - pn.pairs * 16, LANES), F32)
        back = jnp.concatenate([rows_in, pad], 0).T.astype(BF)
        for i in range(pn.per_group):
            lhs_s[pl.ds(pl.multiple_of(src * tw, tw), tw), i * LANES : (i + 1) * LANES] = back[
                i * tw : (i + 1) * tw
            ]
        return carry

    lax.fori_loop(0, nx, unpack, 0)
    which = lax.broadcasted_iota(jnp.int32, (pn.per_group * LANES, 1), 0) % 8

    def pillars(i, carry):
        x_s[i] = dot(lhs_s[...], jnp.where(which == i, ee_s[...], 0.0).astype(BF)).astype(BF)
        return carry

    lax.fori_loop(0, 2 * rows, pillars, 0)

    def row_sample(b, carry):
        y = [
            section(x_s[b * rows + i].astype(F32), g_ref[0:1, :], rqkv_ref, rout_ref).reshape(n // 2, 8, ch)
            for i in range(4)
        ]
        even = [jnp.where(sub, y[i], pltpu.roll(y[i + 1], 4, 1)) for i in (0, 2)]
        odd = [jnp.where(sub, pltpu.roll(y[i], 4, 1), y[i + 1]) for i in (0, 2)]
        s_s[b, :, 0] = jnp.concatenate(even, 1).astype(BF)
        s_s[b, :, 1] = jnp.concatenate(odd, 1).astype(BF)

        def send(t, c):
            to = lax.rem(group + t, n)
            pltpu.make_async_remote_copy(
                src_ref=s_s.at[b, to // 2, lax.rem(to, 2)],
                dst_ref=r_s.at[b, row_group],
                send_sem=row_send.at[b],
                recv_sem=row_recv.at[b],
                device_id=pn.owner(to),
                device_id_type=MESH,
            ).start()
            return c

        lax.fori_loop(1, n, send, 0)
        r_s[b, row_group] = s_s[b, group // 2, lax.rem(group, 2)]
        return carry

    lax.fori_loop(0, 2, row_sample, 0)

    edge = jnp.zeros(cd_s.shape[2:], BF)
    for b in range(2):

        @pl.when(jnp.logical_not(has_left))
        def _():
            cd_s[b, 0] = edge

        @pl.when(jnp.logical_not(has_right))
        def _():
            cd_s[b, cols + 1] = edge

    row = lax.broadcasted_iota(jnp.int32, (pn.height, 1), 0)

    def halo(b, side):
        return pltpu.make_async_remote_copy(
            src_ref=cd_s.at[b, cols if side else 1],
            dst_ref=cd_s.at[b, 0 if side else cols + 1],
            send_sem=hsend.at[b, side],
            recv_sem=hrecv.at[b, side],
            device_id=right if side else left,
            device_id_type=MESH,
        )

    def col_sample(b, carry):
        blocks = r_s.at[b, pl.ds(0, n - 1)]
        pltpu.make_async_copy(blocks, blocks, row_recv.at[b]).wait()
        for i in range(ch // LANES):
            xr_s[i] = r_s[b, :, :, i * LANES : (i + 1) * LANES].astype(F32).reshape(pn.height * cols, LANES)

        def two(u, c):
            for i in range(2):
                at = u if i == 0 else cols - 1 - u
                x = jnp.concatenate(
                    [xr_s[j, pl.ds(at, pn.height, stride=cols), :] for j in range(ch // LANES)], 1
                )
                cd_s[b, at + 1] = section(x, g_ref[1:2, :], cqkv_ref, cout_ref).astype(BF)

            @pl.when(jnp.logical_and(u == 0, has_left))
            def _():
                halo(b, 0).start()

            @pl.when(jnp.logical_and(u == 0, has_right))
            def _():
                halo(b, 1).start()

            return c

        lax.fori_loop(0, cols // 2, two, 0)

        @pl.when(has_left)
        def _():
            halo(b, 1).wait_recv()

        @pl.when(has_right)
        def _():
            halo(b, 0).wait_recv()

        def conv(i, c):
            near = [cd_s[b, i + e].astype(F32) for e in range(3)]
            taps = [sum(near[e] * dk_ref[a, e, :][None] for e in range(3)) for a in range(3)]
            above = jnp.where(row == 0, 0.0, pltpu.roll(taps[0], 1, 0))
            below = jnp.where(row == pn.height - 1, 0.0, pltpu.roll(taps[2], pn.height - 1, 0))
            depth = above + taps[1] + below
            act = (depth / (1.0 + jnp.exp(-depth))).astype(BF)
            o_s[b, i] = (near[1] + dot(act, pw_ref[...])).astype(BF)

            def send(t, cc):
                to = lax.rem(gy + t, ny)
                src = o_s.at[b, i, pl.ds(pl.multiple_of(to * th, th), th)]
                dst = out_ref.at[b * tw + first + i]
                away = jnp.logical_or(t > 0, tile_x != gx)

                @pl.when(away)
                def _():
                    pltpu.make_async_remote_copy(
                        src_ref=src,
                        dst_ref=dst,
                        send_sem=out_sems.at[0],
                        recv_sem=out_sems.at[1],
                        device_id=(to, tile_x),
                        device_id_type=MESH,
                    ).start()

                @pl.when(jnp.logical_not(away))
                def _():
                    pltpu.make_async_copy(src, dst, out_sems.at[2]).start()

                return cc

            lax.fori_loop(0, ny, send, 0)
            return c

        lax.fori_loop(0, cols, conv, 0)
        return carry

    lax.fori_loop(0, 2, col_sample, 0)

    for b in range(2):
        blocks = r_s.at[b, pl.ds(0, n - 1)]
        pltpu.make_async_copy(blocks, blocks, row_send.at[b]).wait()

        @pl.when(has_left)
        def _():
            halo(b, 0).wait_send()

        @pl.when(has_right)
        def _():
            halo(b, 1).wait_send()

    local = tile_x == gx

    def wait_out(count, s):
        part = out_ref.at[pl.ds(0, count)]
        pltpu.make_async_copy(part, part, out_sems.at[s]).wait()

    @pl.when(local)
    def _():
        wait_out(2 * cols * (ny - 1), 0)
        wait_out(2 * cols * (ny - 1), 1)
        wait_out(2 * cols, 2)

    @pl.when(jnp.logical_not(local))
    def _():
        wait_out(2 * cols * ny, 0)
        wait_out(2 * cols * ny, 1)


def per_device(
    occupancy,
    counts,
    level_embed,
    count_weight,
    norm_gains,
    row_qkv,
    row_out,
    col_qkv,
    col_out,
    depth_kernel,
    point_weight,
):
    ny, nx = lax.axis_size("gy"), lax.axis_size("gx")
    th, tw = counts.shape[1:]
    ch = level_embed.shape[1]
    pn = Plan(ny, nx, th * ny, tw * nx)
    vmem = pl.BlockSpec(memory_space=pltpu.VMEM)
    out = pl.pallas_call(
        functools.partial(kernel, pn),
        out_shape=jax.ShapeDtypeStruct((2 * tw, th, ch), BF),
        in_specs=[vmem] * 11,
        out_specs=pl.BlockSpec(memory_space=pl.ANY),
        scratch_shapes=[
            pltpu.VMEM((nx, pn.pairs, 16, LANES), BF),
            pltpu.VMEM((nx, pn.pairs, 16, LANES), BF),
            pltpu.VMEM((pn.width, pn.per_group * LANES), BF),
            pltpu.VMEM((pn.per_group * LANES, ch), F32),
            pltpu.VMEM((2 * pn.rows, pn.width, ch), BF),
            pltpu.VMEM((2, pn.n // 2, 2, 16, ch), BF),
            pltpu.VMEM((2, pn.n, 16, ch), BF),
            pltpu.VMEM((ch // LANES, pn.height * pn.cols, LANES), F32),
            pltpu.VMEM((2, pn.cols + 2, pn.height, ch), BF),
            pltpu.VMEM((2, pn.cols, pn.height, ch), BF),
            pltpu.SemaphoreType.DMA((2,)),
            pltpu.SemaphoreType.DMA((2,)),
            pltpu.SemaphoreType.DMA((2,)),
            pltpu.SemaphoreType.DMA((2, 2)),
            pltpu.SemaphoreType.DMA((2, 2)),
            pltpu.SemaphoreType.DMA((3,)),
        ],
        compiler_params=pltpu.CompilerParams(
            collective_id=0, has_side_effects=True, vmem_limit_bytes=60 * 2**20
        ),
        name="block",
    )(
        occupancy.transpose(0, 1, 3, 2),
        counts.transpose(0, 2, 1),
        level_embed,
        count_weight[None],
        norm_gains,
        row_qkv,
        row_out,
        col_qkv,
        col_out,
        depth_kernel,
        point_weight,
    )
    return out.reshape(2, tw, th, ch).transpose(0, 2, 1, 3)


def solution(mesh):
    in_specs = (P(None, None, "gy", "gx"), P(None, "gy", "gx")) + (P(),) * 9
    out_specs = P(None, "gy", "gx", None)
    return jax.shard_map(
        per_device, mesh=mesh, in_specs=in_specs, out_specs=out_specs, check_vma=False
    )
```

```python
import functools

import jax
import jax.numpy as jnp
from jax import lax
from jax.experimental import pallas as pl
from jax.experimental.pallas import tpu as pltpu
from jax.sharding import PartitionSpec as P

HEADS = 8
BF = jnp.bfloat16
F32 = jnp.float32
LOG2E = 1.4426950408889634
MESH = pl.DeviceIdType.MESH
DEPTH = 48
LANES = 128


def dot(a, b):
    return jnp.dot(a, b, preferred_element_type=F32)


def section(x, gain, wqkv_ref, wout_ref):
    length, ch = x.shape
    half_ch = ch // 2
    head_dim = ch // HEADS
    cen = x - jnp.mean(x, -1, keepdims=True)
    var = jnp.mean(cen * cen, -1, keepdims=True)
    normed = (cen * lax.rsqrt(var + 1e-5) * gain).astype(BF)
    q = (dot(normed, wqkv_ref[:, :ch]) * (LOG2E * head_dim ** -0.5)).astype(BF)
    k = dot(normed, wqkv_ref[:, ch : 2 * ch]).astype(BF)
    v = dot(normed, wqkv_ref[:, 2 * ch :]).astype(BF)
    ones = jnp.ones((length, half_ch), BF)
    lane = lax.broadcasted_iota(jnp.int32, (1, ch), 1) // head_dim
    halves = []
    for half in range(2):
        num = den = None
        vals = jnp.concatenate([v[:, half * half_ch : (half + 1) * half_ch], ones], 1)
        for head in range(half * HEADS // 2, (half + 1) * HEADS // 2):
            qm = jnp.where(lane == head, q, BF(0))
            s = lax.dot_general(qm, k, (((1,), (1,)), ((), ())), preferred_element_type=F32)
            e = jnp.exp2(s - jnp.max(s, -1, keepdims=True)).astype(BF)
            r = dot(e, vals)
            if num is None:
                num, den = r[:, :half_ch], r[:, half_ch:]
            else:
                mine = lane[:, half * half_ch : (half + 1) * half_ch] == head
                num = jnp.where(mine, r[:, :half_ch], num)
                den = jnp.where(mine, r[:, half_ch:], den)
        halves.append((num / den).astype(BF))
    return x + dot(jnp.concatenate(halves, 1), wout_ref[...])


def split3(x):
    a = x.astype(BF).astype(F32)
    b = (x - a).astype(BF).astype(F32)
    return a, b, x - a - b


class Plan:
    def __init__(self, ny, nx, height, width):
        self.ny, self.nx = ny, nx
        self.n = ny * nx
        self.height, self.width = height, width
        self.th, self.tw = height // ny, width // nx
        self.rows = height // self.n
        self.cols = width // self.n
        self.per_group = LANES // self.tw
        self.pairs = DEPTH // self.per_group // 2

    def snake(self, q):
        return jnp.where(q < self.ny // 2, q, 3 * self.ny // 2 - 1 - q)

    def owner(self, group):
        m = lax.rem(group, 2 * self.ny)
        return (self.snake(m // 2), 2 * (group // (2 * self.ny)) + lax.rem(m, 2))


def kernel(
    pn,
    occ_ref, cnt_ref, emb_ref, cw_ref, g_ref, rqkv_ref, rout_ref, cqkv_ref, cout_ref, dk_ref, pw_ref,
    out_ref,
    snd_s, got_s, lhs_s, ee_s, x_s, s_s, r_s, xr_s, cd_s, o_s,
    all_in, occ_sems, row_send, row_recv, hsend, hrecv, out_sems,
):
    ny, nx, n = pn.ny, pn.nx, pn.n
    th, tw, rows, cols = pn.th, pn.tw, pn.rows, pn.cols
    ch = emb_ref.shape[1]
    levels = emb_ref.shape[0]
    gy, gx = lax.axis_index("gy"), lax.axis_index("gx")
    core = lax.rem(gx, 2)
    m = 2 * pn.snake(gy) + core
    group = (gx // 2) * (2 * ny) + m
    row_group = gy * nx + gx
    tile_x = 2 * (gx // 2) + m // ny
    first = lax.rem(m, ny) * cols
    has_left, has_right = group > 0, group < n - 1
    left = pn.owner(jnp.maximum(group - 1, 0))
    right = pn.owner(jnp.minimum(group + 1, n - 1))
    barrier = pltpu.get_barrier_semaphore()

    def greet(sem, along_x):
        def one(t, carry):
            other = (gy, lax.rem(gx + t, nx)) if along_x else (lax.rem(gy + t, ny), gx)
            pl.semaphore_signal(sem, inc=1, device_id=other, device_id_type=MESH)
            return carry

        lax.fori_loop(1, nx if along_x else ny, one, 0)

    greet(barrier, True)
    greet(barrier, False)

    def lined_up(b):
        logs = split3(jnp.log1p(cnt_ref[b].astype(F32)))
        terms = [logs[i] for i in (0, 0, 0, 1, 1, 2)]
        return jnp.concatenate(
            [occ_ref[b].astype(F32).reshape(levels * tw, th)]
            + terms
            + [jnp.zeros(((DEPTH - levels - len(terms)) * tw, th), F32)],
            0,
        )

    turned = jnp.concatenate([lined_up(0), lined_up(1)], 1).T
    t0 = turned[:th].reshape(th // 8, 8, DEPTH * tw)
    t1 = turned[th:].reshape(th // 8, 8, DEPTH * tw)
    sub = lax.broadcasted_iota(jnp.int32, (1, 8, 1), 1) < 4
    both = (jnp.where(sub, t0, pltpu.roll(t1, 4, 1)), jnp.where(sub, pltpu.roll(t0, 4, 1), t1))
    for t in range(th // 8):
        for i in range(2):
            for p in range(pn.pairs):
                part = both[i][t][:, 2 * p * LANES : 2 * (p + 1) * LANES]
                snd_s[2 * t + i, p] = jnp.concatenate([part[:, :LANES], part[:, LANES:]], 0).astype(BF)

    pl.semaphore_wait(barrier, nx - 1 + ny - 1)

    def send_occ(t, carry):
        to = lax.rem(gx + t, nx)
        pltpu.make_async_remote_copy(
            src_ref=snd_s.at[to],
            dst_ref=got_s.at[gx],
            send_sem=occ_sems.at[0],
            recv_sem=occ_sems.at[1],
            device_id=(gy, to),
            device_id_type=MESH,
        ).start()
        return carry

    lax.fori_loop(1, nx, send_occ, 0)
    got_s[gx] = snd_s[gx]
    greet(all_in, False)

    w1, w2, w3 = split3(cw_ref[...])
    table = [emb_ref[i : i + 1, :].astype(F32) for i in range(levels)] + [w1, w2, w3, w1, w2, w1]
    zero = jnp.zeros((8, ch), F32)
    for i in range(pn.per_group):
        for j in range(LANES // 8):
            at = j * pn.per_group + i
            r0 = i * LANES + j * 8
            ee_s[r0 : r0 + 8, :] = jnp.broadcast_to(table[at], (8, ch)) if at < len(table) else zero

    for s in range(2):
        arrived = got_s.at[pl.ds(0, nx - 1)]
        pltpu.make_async_copy(arrived, arrived, occ_sems.at[s]).wait()

    def unpack(src, carry):
        rows_in = got_s[src].reshape(pn.pairs * 16, LANES).astype(F32)
        pad = jnp.zeros((LANES - pn.pairs * 16, LANES), F32)
        back = jnp.concatenate([rows_in, pad], 0).T.astype(BF)
        for i in range(pn.per_group):
            lhs_s[pl.ds(pl.multiple_of(src * tw, tw), tw), i * LANES : (i + 1) * LANES] = back[
                i * tw : (i + 1) * tw
            ]
        return carry

    lax.fori_loop(0, nx, unpack, 0, unroll=16)
    which = lax.broadcasted_iota(jnp.int32, (pn.per_group * LANES, 1), 0) % 8

    def pillars(i, carry):
        x_s[i] = dot(lhs_s[...], jnp.where(which == i, ee_s[...], 0.0).astype(BF)).astype(BF)
        return carry

    lax.fori_loop(0, 2 * rows, pillars, 0, unroll=2)
    pl.semaphore_wait(all_in, ny - 1)

    def row_sample(b, carry):
        y = [
            section(x_s[b * rows + i].astype(F32), g_ref[0:1, :], rqkv_ref, rout_ref).reshape(n // 2, 8, ch)
            for i in range(4)
        ]
        even = [jnp.where(sub, y[i], pltpu.roll(y[i + 1], 4, 1)) for i in (0, 2)]
        odd = [jnp.where(sub, pltpu.roll(y[i], 4, 1), y[i + 1]) for i in (0, 2)]
        s_s[b, :, 0] = jnp.concatenate(even, 1).astype(BF)
        s_s[b, :, 1] = jnp.concatenate(odd, 1).astype(BF)

        def send(t):
            to = lax.rem(group + 37 * t, n)
            pltpu.make_async_remote_copy(
                src_ref=s_s.at[b, to // 2, lax.rem(to, 2)],
                dst_ref=r_s.at[b, row_group],
                send_sem=row_send.at[b],
                recv_sem=row_recv.at[b],
                device_id=pn.owner(to),
                device_id_type=MESH,
            ).start()

        def send_some(t, c):
            for i in range(7):
                send(t * 7 + i + 1)
            return c

        lax.fori_loop(0, (n - 1) // 7, send_some, 0)
        for t in range((n - 1) // 7 * 7 + 1, n):
            send(t)
        r_s[b, row_group] = s_s[b, group // 2, lax.rem(group, 2)]
        return carry

    lax.fori_loop(0, 2, row_sample, 0)

    edge = jnp.zeros(cd_s.shape[2:], BF)
    for b in range(2):

        @pl.when(jnp.logical_not(has_left))
        def _():
            cd_s[b, 0] = edge

        @pl.when(jnp.logical_not(has_right))
        def _():
            cd_s[b, cols + 1] = edge

    row = lax.broadcasted_iota(jnp.int32, (pn.height, 1), 0)

    def halo(b, side):
        return pltpu.make_async_remote_copy(
            src_ref=cd_s.at[b, cols if side else 1],
            dst_ref=cd_s.at[b, 0 if side else cols + 1],
            send_sem=hsend.at[b, side],
            recv_sem=hrecv.at[b, side],
            device_id=right if side else left,
            device_id_type=MESH,
        )

    def col_sample(b, carry):
        blocks = r_s.at[b, pl.ds(0, n - 1)]
        pltpu.make_async_copy(blocks, blocks, row_recv.at[b]).wait()
        for i in range(ch // LANES):
            xr_s[i] = r_s[b, :, :, i * LANES : (i + 1) * LANES].astype(F32).reshape(pn.height * cols, LANES)

        def line(at):
            x = jnp.concatenate(
                [xr_s[j, pl.ds(at, pn.height, stride=cols), :] for j in range(ch // LANES)], 1
            )
            cd_s[b, at + 1] = section(x, g_ref[1:2, :], cqkv_ref, cout_ref).astype(BF)

        def conv(i, c):
            near = [cd_s[b, i + e].astype(F32) for e in range(3)]
            taps = [sum(near[e] * dk_ref[a, e, :][None] for e in range(3)) for a in range(3)]
            above = jnp.where(row == 0, 0.0, pltpu.roll(taps[0], 1, 0))
            below = jnp.where(row == pn.height - 1, 0.0, pltpu.roll(taps[2], pn.height - 1, 0))
            depth = above + taps[1] + below
            act = (depth / (1.0 + jnp.exp(-depth))).astype(BF)
            o_s[b, i] = (near[1] + dot(act, pw_ref[...])).astype(BF)

            def send(t, cc):
                to = lax.rem(gy + 3 * t, ny)
                src = o_s.at[b, i, pl.ds(pl.multiple_of(to * th, th), th)]
                dst = out_ref.at[b * tw + first + i]
                away = jnp.logical_or(t > 0, tile_x != gx)

                @pl.when(away)
                def _():
                    pltpu.make_async_remote_copy(
                        src_ref=src,
                        dst_ref=dst,
                        send_sem=out_sems.at[0],
                        recv_sem=out_sems.at[1],
                        device_id=(to, tile_x),
                        device_id_type=MESH,
                    ).start()

                @pl.when(jnp.logical_not(away))
                def _():
                    pltpu.make_async_copy(src, dst, out_sems.at[2]).start()

                return cc

            lax.fori_loop(0, ny, send, 0)
            return c

        line(0)
        line(cols - 1)

        @pl.when(has_left)
        def _():
            halo(b, 0).start()

        @pl.when(has_right)
        def _():
            halo(b, 1).start()

        line(1)

        @pl.when(has_left)
        def _():
            halo(b, 1).wait_recv()

        @pl.when(has_right)
        def _():
            halo(b, 0).wait_recv()

        def last_two(i, c):
            @pl.when(i == 1)
            def _():
                line(2)

            conv(i, 0)
            return c

        lax.fori_loop(0, cols, last_two, 0)
        return carry

    lax.fori_loop(0, 2, col_sample, 0)

    for b in range(2):
        blocks = r_s.at[b, pl.ds(0, n - 1)]
        pltpu.make_async_copy(blocks, blocks, row_send.at[b]).wait()

        @pl.when(has_left)
        def _():
            halo(b, 0).wait_send()

        @pl.when(has_right)
        def _():
            halo(b, 1).wait_send()

    local = tile_x == gx

    def wait_out(count, s):
        part = out_ref.at[pl.ds(0, count)]
        pltpu.make_async_copy(part, part, out_sems.at[s]).wait()

    @pl.when(local)
    def _():
        wait_out(2 * cols * (ny - 1), 0)
        wait_out(2 * cols * (ny - 1), 1)
        wait_out(2 * cols, 2)

    @pl.when(jnp.logical_not(local))
    def _():
        wait_out(2 * cols * ny, 0)
        wait_out(2 * cols * ny, 1)


def per_device(
    occupancy,
    counts,
    level_embed,
    count_weight,
    norm_gains,
    row_qkv,
    row_out,
    col_qkv,
    col_out,
    depth_kernel,
    point_weight,
):
    ny, nx = lax.axis_size("gy"), lax.axis_size("gx")
    th, tw = counts.shape[1:]
    ch = level_embed.shape[1]
    pn = Plan(ny, nx, th * ny, tw * nx)
    vmem = pl.BlockSpec(memory_space=pltpu.VMEM)
    out = pl.pallas_call(
        functools.partial(kernel, pn),
        out_shape=jax.ShapeDtypeStruct((2 * tw, th, ch), BF),
        in_specs=[vmem] * 11,
        out_specs=pl.BlockSpec(memory_space=pl.ANY),
        scratch_shapes=[
            pltpu.VMEM((nx, pn.pairs, 16, LANES), BF),
            pltpu.VMEM((nx, pn.pairs, 16, LANES), BF),
            pltpu.VMEM((pn.width, pn.per_group * LANES), BF),
            pltpu.VMEM((pn.per_group * LANES, ch), F32),
            pltpu.VMEM((2 * pn.rows, pn.width, ch), BF),
            pltpu.VMEM((2, pn.n // 2, 2, 16, ch), BF),
            pltpu.VMEM((2, pn.n, 16, ch), BF),
            pltpu.VMEM((ch // LANES, pn.height * pn.cols, LANES), F32),
            pltpu.VMEM((2, pn.cols + 2, pn.height, ch), BF),
            pltpu.VMEM((2, pn.cols, pn.height, ch), BF),
            pltpu.SemaphoreType.REGULAR,
            pltpu.SemaphoreType.DMA((2,)),
            pltpu.SemaphoreType.DMA((2,)),
            pltpu.SemaphoreType.DMA((2,)),
            pltpu.SemaphoreType.DMA((2, 2)),
            pltpu.SemaphoreType.DMA((2, 2)),
            pltpu.SemaphoreType.DMA((3,)),
        ],
        compiler_params=pltpu.CompilerParams(
            collective_id=0, has_side_effects=True, vmem_limit_bytes=60 * 2**20
        ),
        name="block",
    )(
        occupancy.transpose(0, 1, 3, 2),
        counts.transpose(0, 2, 1),
        level_embed,
        count_weight[None],
        norm_gains,
        row_qkv,
        row_out,
        col_qkv,
        col_out,
        depth_kernel,
        point_weight,
    )
    return out.reshape(2, tw, th, ch).transpose(0, 2, 1, 3)


def solution(mesh):
    in_specs = (P(None, None, "gy", "gx"), P(None, "gy", "gx")) + (P(),) * 9
    out_specs = P(None, "gy", "gx", None)
    return jax.shard_map(
        per_device, mesh=mesh, in_specs=in_specs, out_specs=out_specs, check_vma=False
    )
```

```python
import functools

import jax
import jax.numpy as jnp
from jax import lax
from jax.experimental import pallas as pl
from jax.experimental.pallas import tpu as pltpu
from jax.sharding import PartitionSpec as P

HEADS = 8
BF = jnp.bfloat16
F32 = jnp.float32
LOG2E = 1.4426950408889634
MESH = pl.DeviceIdType.MESH
DEPTH = 48
LANES = 128


def dot(a, b):
    return jnp.dot(a, b, preferred_element_type=F32)


def section(x, gain, wqkv_ref, wout_ref):
    length, ch = x.shape
    half_ch = ch // 2
    head_dim = ch // HEADS
    cen = x - jnp.mean(x, -1, keepdims=True)
    var = jnp.mean(cen * cen, -1, keepdims=True)
    normed = (cen * lax.rsqrt(var + 1e-5) * gain).astype(BF)
    q = (dot(normed, wqkv_ref[:, :ch]) * (LOG2E * head_dim ** -0.5)).astype(BF)
    k = dot(normed, wqkv_ref[:, ch : 2 * ch]).astype(BF)
    v = dot(normed, wqkv_ref[:, 2 * ch :]).astype(BF)
    ones = jnp.ones((length, half_ch), BF)
    lane = lax.broadcasted_iota(jnp.int32, (1, ch), 1) // head_dim
    halves = []
    for half in range(2):
        num = den = None
        vals = jnp.concatenate([v[:, half * half_ch : (half + 1) * half_ch], ones], 1)
        for head in range(half * HEADS // 2, (half + 1) * HEADS // 2):
            qm = jnp.where(lane == head, q, BF(0))
            s = lax.dot_general(qm, k, (((1,), (1,)), ((), ())), preferred_element_type=F32)
            e = jnp.exp2(s - jnp.max(s, -1, keepdims=True)).astype(BF)
            r = dot(e, vals)
            if num is None:
                num, den = r[:, :half_ch], r[:, half_ch:]
            else:
                mine = lane[:, half * half_ch : (half + 1) * half_ch] == head
                num = jnp.where(mine, r[:, :half_ch], num)
                den = jnp.where(mine, r[:, half_ch:], den)
        halves.append((num / den).astype(BF))
    return x + dot(jnp.concatenate(halves, 1), wout_ref[...])


def split3(x):
    a = x.astype(BF).astype(F32)
    b = (x - a).astype(BF).astype(F32)
    return a, b, x - a - b


class Plan:
    def __init__(self, ny, nx, height, width):
        self.ny, self.nx = ny, nx
        self.n = ny * nx
        self.height, self.width = height, width
        self.th, self.tw = height // ny, width // nx
        self.rows = height // self.n
        self.cols = width // self.n
        self.per_group = LANES // self.tw
        self.pairs = DEPTH // self.per_group // 2

    def snake(self, q):
        return jnp.where(q < self.ny // 2, q, 3 * self.ny // 2 - 1 - q)

    def owner(self, group):
        m = lax.rem(group, 2 * self.ny)
        return (self.snake(m // 2), 2 * (group // (2 * self.ny)) + lax.rem(m, 2))


def kernel(
    pn,
    occ_ref, cnt_ref, emb_ref, cw_ref, g_ref, rqkv_ref, rout_ref, cqkv_ref, cout_ref, dk_ref, pw_ref,
    out_ref,
    snd_s, got_s, lhs_s, ee_s, x_s, s_s, r_s, xr_s, cd_s, o_s,
    all_in, occ_sems, row_send, row_recv, hsend, hrecv, out_sems,
):
    ny, nx, n = pn.ny, pn.nx, pn.n
    th, tw, rows, cols = pn.th, pn.tw, pn.rows, pn.cols
    ch = emb_ref.shape[1]
    levels = emb_ref.shape[0]
    gy, gx = lax.axis_index("gy"), lax.axis_index("gx")
    core = lax.rem(gx, 2)
    m = 2 * pn.snake(gy) + core
    group = (gx // 2) * (2 * ny) + m
    row_group = gy * nx + gx
    tile_x = 2 * (gx // 2) + m // ny
    first = lax.rem(m, ny) * cols
    has_left, has_right = group > 0, group < n - 1
    left = pn.owner(jnp.maximum(group - 1, 0))
    right = pn.owner(jnp.minimum(group + 1, n - 1))
    barrier = pltpu.get_barrier_semaphore()

    def greet(sem, along_x):
        def one(t, carry):
            other = (gy, lax.rem(gx + t, nx)) if along_x else (lax.rem(gy + t, ny), gx)
            pl.semaphore_signal(sem, inc=1, device_id=other, device_id_type=MESH)
            return carry

        lax.fori_loop(1, nx if along_x else ny, one, 0)

    greet(barrier, True)
    greet(barrier, False)

    def lined_up(b):
        logs = split3(jnp.log1p(cnt_ref[b].astype(F32)))
        terms = [logs[i] for i in (0, 0, 0, 1, 1, 2)]
        return jnp.concatenate(
            [occ_ref[b].astype(F32).reshape(levels * tw, th)]
            + terms
            + [jnp.zeros(((DEPTH - levels - len(terms)) * tw, th), F32)],
            0,
        )

    turned = jnp.concatenate([lined_up(0), lined_up(1)], 1).T
    t0 = turned[:th].reshape(th // 8, 8, DEPTH * tw)
    t1 = turned[th:].reshape(th // 8, 8, DEPTH * tw)
    sub = lax.broadcasted_iota(jnp.int32, (1, 8, 1), 1) < 4
    both = (jnp.where(sub, t0, pltpu.roll(t1, 4, 1)), jnp.where(sub, pltpu.roll(t0, 4, 1), t1))
    for t in range(th // 8):
        for i in range(2):
            for p in range(pn.pairs):
                part = both[i][t][:, 2 * p * LANES : 2 * (p + 1) * LANES]
                snd_s[2 * t + i, p] = jnp.concatenate([part[:, :LANES], part[:, LANES:]], 0).astype(BF)

    pl.semaphore_wait(barrier, nx - 1 + ny - 1)

    def send_occ(t, carry):
        to = lax.rem(gx + t, nx)
        pltpu.make_async_remote_copy(
            src_ref=snd_s.at[to],
            dst_ref=got_s.at[gx],
            send_sem=occ_sems.at[0],
            recv_sem=occ_sems.at[1],
            device_id=(gy, to),
            device_id_type=MESH,
        ).start()
        return carry

    lax.fori_loop(1, nx, send_occ, 0)
    got_s[gx] = snd_s[gx]
    greet(all_in, False)

    w1, w2, w3 = split3(cw_ref[...])
    table = [emb_ref[i : i + 1, :].astype(F32) for i in range(levels)] + [w1, w2, w3, w1, w2, w1]
    zero = jnp.zeros((8, ch), F32)
    for i in range(pn.per_group):
        for j in range(LANES // 8):
            at = j * pn.per_group + i
            r0 = i * LANES + j * 8
            ee_s[r0 : r0 + 8, :] = jnp.broadcast_to(table[at], (8, ch)) if at < len(table) else zero

    for s in range(2):
        arrived = got_s.at[pl.ds(0, nx - 1)]
        pltpu.make_async_copy(arrived, arrived, occ_sems.at[s]).wait()

    def unpack(src, carry):
        rows_in = got_s[src].reshape(pn.pairs * 16, LANES).astype(F32)
        pad = jnp.zeros((LANES - pn.pairs * 16, LANES), F32)
        back = jnp.concatenate([rows_in, pad], 0).T.astype(BF)
        for i in range(pn.per_group):
            lhs_s[pl.ds(pl.multiple_of(src * tw, tw), tw), i * LANES : (i + 1) * LANES] = back[
                i * tw : (i + 1) * tw
            ]
        return carry

    lax.fori_loop(0, nx, unpack, 0, unroll=16)
    which = lax.broadcasted_iota(jnp.int32, (pn.per_group * LANES, 1), 0) % 8

    def pillars(i, carry):
        x_s[i] = dot(lhs_s[...], jnp.where(which == i, ee_s[...], 0.0).astype(BF)).astype(BF)
        return carry

    lax.fori_loop(0, 2 * rows, pillars, 0, unroll=2)
    pl.semaphore_wait(all_in, ny - 1)

    def row_sample(b, carry):
        y = [
            section(x_s[b * rows + i].astype(F32), g_ref[0:1, :], rqkv_ref, rout_ref).reshape(n // 2, 8, ch)
            for i in range(4)
        ]
        even = [jnp.where(sub, y[i], pltpu.roll(y[i + 1], 4, 1)) for i in (0, 2)]
        odd = [jnp.where(sub, pltpu.roll(y[i], 4, 1), y[i + 1]) for i in (0, 2)]
        s_s[b, :, 0] = jnp.concatenate(even, 1).astype(BF)
        s_s[b, :, 1] = jnp.concatenate(odd, 1).astype(BF)

        def send(t):
            u = lax.rem(37 * t + gy * nx + gx, n)
            to_y, to_x = lax.div(u, nx), lax.rem(u, nx)
            q = pn.snake(to_y)
            pltpu.make_async_remote_copy(
                src_ref=s_s.at[b, lax.div(to_x, 2) * ny + q, lax.rem(to_x, 2)],
                dst_ref=r_s.at[b, row_group],
                send_sem=row_send.at[b],
                recv_sem=row_recv.at[b],
                device_id=(to_y, to_x),
                device_id_type=MESH,
            ).start()

        def send_some(t, c):
            for i in range(7):
                send(t * 7 + i + 1)
            return c

        lax.fori_loop(0, (n - 1) // 7, send_some, 0)
        for t in range((n - 1) // 7 * 7 + 1, n):
            send(t)
        r_s[b, row_group] = s_s[b, group // 2, lax.rem(group, 2)]
        return carry

    lax.fori_loop(0, 2, row_sample, 0)

    edge = jnp.zeros(cd_s.shape[2:], BF)
    for b in range(2):

        @pl.when(jnp.logical_not(has_left))
        def _():
            cd_s[b, 0] = edge

        @pl.when(jnp.logical_not(has_right))
        def _():
            cd_s[b, cols + 1] = edge

    row = lax.broadcasted_iota(jnp.int32, (pn.height, 1), 0)

    def halo(b, side):
        return pltpu.make_async_remote_copy(
            src_ref=cd_s.at[b, cols if side else 1],
            dst_ref=cd_s.at[b, 0 if side else cols + 1],
            send_sem=hsend.at[b, side],
            recv_sem=hrecv.at[b, side],
            device_id=right if side else left,
            device_id_type=MESH,
        )

    def col_sample(b, carry):
        blocks = r_s.at[b, pl.ds(0, n - 1)]
        pltpu.make_async_copy(blocks, blocks, row_recv.at[b]).wait()
        for i in range(ch // LANES):
            xr_s[i] = r_s[b, :, :, i * LANES : (i + 1) * LANES].astype(F32).reshape(pn.height * cols, LANES)

        def line(at):
            x = jnp.concatenate(
                [xr_s[j, pl.ds(at, pn.height, stride=cols), :] for j in range(ch // LANES)], 1
            )
            cd_s[b, at + 1] = section(x, g_ref[1:2, :], cqkv_ref, cout_ref).astype(BF)

        def conv(i, c):
            near = [cd_s[b, i + e].astype(F32) for e in range(3)]
            taps = [sum(near[e] * dk_ref[a, e, :][None] for e in range(3)) for a in range(3)]
            above = jnp.where(row == 0, 0.0, pltpu.roll(taps[0], 1, 0))
            below = jnp.where(row == pn.height - 1, 0.0, pltpu.roll(taps[2], pn.height - 1, 0))
            depth = above + taps[1] + below
            act = (depth / (1.0 + jnp.exp(-depth))).astype(BF)
            o_s[b, i] = (near[1] + dot(act, pw_ref[...])).astype(BF)

            def send(t, cc):
                to = lax.rem(gy + 3 * t, ny)
                src = o_s.at[b, i, pl.ds(pl.multiple_of(to * th, th), th)]
                dst = out_ref.at[b * tw + first + i]
                away = jnp.logical_or(t > 0, tile_x != gx)

                @pl.when(away)
                def _():
                    pltpu.make_async_remote_copy(
                        src_ref=src,
                        dst_ref=dst,
                        send_sem=out_sems.at[0],
                        recv_sem=out_sems.at[1],
                        device_id=(to, tile_x),
                        device_id_type=MESH,
                    ).start()

                @pl.when(jnp.logical_not(away))
                def _():
                    pltpu.make_async_copy(src, dst, out_sems.at[2]).start()

                return cc

            lax.fori_loop(0, ny, send, 0)
            return c

        line(0)

        @pl.when(has_left)
        def _():
            halo(b, 0).start()

        line(1)
        line(2)

        def last_lines(i, c):
            @pl.when(i == 1)
            def _():
                line(3)

                @pl.when(has_right)
                def _():
                    halo(b, 1).start()

            @pl.when(jnp.logical_and(i == 2, has_right))
            def _():
                halo(b, 0).wait_recv()

            @pl.when(jnp.logical_and(i == 3, has_left))
            def _():
                halo(b, 1).wait_recv()

            conv(lax.rem(i + 1, cols), 0)
            return c

        lax.fori_loop(0, cols, last_lines, 0)
        return carry

    lax.fori_loop(0, 2, col_sample, 0)

    for b in range(2):
        blocks = r_s.at[b, pl.ds(0, n - 1)]
        pltpu.make_async_copy(blocks, blocks, row_send.at[b]).wait()

        @pl.when(has_left)
        def _():
            halo(b, 0).wait_send()

        @pl.when(has_right)
        def _():
            halo(b, 1).wait_send()

    local = tile_x == gx

    def wait_out(count, s):
        part = out_ref.at[pl.ds(0, count)]
        pltpu.make_async_copy(part, part, out_sems.at[s]).wait()

    @pl.when(local)
    def _():
        wait_out(2 * cols * (ny - 1), 0)
        wait_out(2 * cols * (ny - 1), 1)
        wait_out(2 * cols, 2)

    @pl.when(jnp.logical_not(local))
    def _():
        wait_out(2 * cols * ny, 0)
        wait_out(2 * cols * ny, 1)


def turn_kernel(parts, x_ref, o_ref, x_s, o_s, in_sems, out_sems):
    samples, _, th, _ = x_ref.shape
    step = th // parts

    def bring(b, i):
        rows = pl.ds(i * step, step)
        return pltpu.make_async_copy(x_ref.at[b, :, rows], x_s.at[b, :, rows], in_sems.at[b, i])

    def leave(b, i):
        rows = pl.ds(i * step, step)
        return pltpu.make_async_copy(o_s.at[b, rows], o_ref.at[b, rows], out_sems.at[b, i])

    order = [(b, i) for b in range(samples) for i in range(parts)]
    for at in order:
        bring(*at).start()
    for b, i in order:
        bring(b, i).wait()
        o_s[b, i * step : (i + 1) * step] = jnp.swapaxes(x_s[b, :, i * step : (i + 1) * step], 0, 1)
        leave(b, i).start()
    for at in order:
        leave(*at).wait()


def turn(x, parts):
    samples, tw, th, ch = x.shape
    return pl.pallas_call(
        functools.partial(turn_kernel, parts),
        in_specs=[pl.BlockSpec(memory_space=pl.ANY)],
        out_specs=pl.BlockSpec(memory_space=pl.ANY),
        out_shape=jax.ShapeDtypeStruct((samples, th, tw, ch), x.dtype),
        scratch_shapes=[
            pltpu.VMEM(x.shape, x.dtype),
            pltpu.VMEM((samples, th, tw, ch), x.dtype),
            pltpu.SemaphoreType.DMA((samples, parts)),
            pltpu.SemaphoreType.DMA((samples, parts)),
        ],
        compiler_params=pltpu.CompilerParams(vmem_limit_bytes=60 * 2**20),
        name="turn",
    )(x)


def per_device(
    occupancy,
    counts,
    level_embed,
    count_weight,
    norm_gains,
    row_qkv,
    row_out,
    col_qkv,
    col_out,
    depth_kernel,
    point_weight,
):
    ny, nx = lax.axis_size("gy"), lax.axis_size("gx")
    th, tw = counts.shape[1:]
    ch = level_embed.shape[1]
    pn = Plan(ny, nx, th * ny, tw * nx)
    vmem = pl.BlockSpec(memory_space=pltpu.VMEM)
    out = pl.pallas_call(
        functools.partial(kernel, pn),
        out_shape=jax.ShapeDtypeStruct((2 * tw, th, ch), BF),
        in_specs=[vmem] * 11,
        out_specs=pl.BlockSpec(memory_space=pl.ANY),
        scratch_shapes=[
            pltpu.VMEM((nx, pn.pairs, 16, LANES), BF),
            pltpu.VMEM((nx, pn.pairs, 16, LANES), BF),
            pltpu.VMEM((pn.width, pn.per_group * LANES), BF),
            pltpu.VMEM((pn.per_group * LANES, ch), F32),
            pltpu.VMEM((2 * pn.rows, pn.width, ch), BF),
            pltpu.VMEM((2, pn.n // 2, 2, 16, ch), BF),
            pltpu.VMEM((2, pn.n, 16, ch), BF),
            pltpu.VMEM((ch // LANES, pn.height * pn.cols, LANES), F32),
            pltpu.VMEM((2, pn.cols + 2, pn.height, ch), BF),
            pltpu.VMEM((2, pn.cols, pn.height, ch), BF),
            pltpu.SemaphoreType.REGULAR,
            pltpu.SemaphoreType.DMA((2,)),
            pltpu.SemaphoreType.DMA((2,)),
            pltpu.SemaphoreType.DMA((2,)),
            pltpu.SemaphoreType.DMA((2, 2)),
            pltpu.SemaphoreType.DMA((2, 2)),
            pltpu.SemaphoreType.DMA((3,)),
        ],
        compiler_params=pltpu.CompilerParams(
            collective_id=0, has_side_effects=True, vmem_limit_bytes=60 * 2**20
        ),
        name="block",
    )(
        occupancy.transpose(0, 1, 3, 2),
        counts.transpose(0, 2, 1),
        level_embed,
        count_weight[None],
        norm_gains,
        row_qkv,
        row_out,
        col_qkv,
        col_out,
        depth_kernel,
        point_weight,
    )
    return turn(out.reshape(2, tw, th, ch), 2)


def solution(mesh):
    in_specs = (P(None, None, "gy", "gx"), P(None, "gy", "gx")) + (P(),) * 9
    out_specs = P(None, "gy", "gx", None)
    return jax.shard_map(
        per_device, mesh=mesh, in_specs=in_specs, out_specs=out_specs, check_vma=False
    )
```

```python
import functools

import jax
import jax.numpy as jnp
from jax import lax
from jax.experimental import pallas as pl
from jax.experimental.pallas import tpu as pltpu
from jax.sharding import PartitionSpec as P

HEADS = 8
BF = jnp.bfloat16
F32 = jnp.float32
LOG2E = 1.4426950408889634
MESH = pl.DeviceIdType.MESH
DEPTH = 48
LANES = 128


def dot(a, b):
    return jnp.dot(a, b, preferred_element_type=F32)


def section(x, gain, wqkv_ref, wout_ref):
    length, ch = x.shape
    half_ch = ch // 2
    head_dim = ch // HEADS
    cen = x - jnp.mean(x, -1, keepdims=True)
    var = jnp.mean(cen * cen, -1, keepdims=True)
    normed = (cen * lax.rsqrt(var + 1e-5) * gain).astype(BF)
    q = (dot(normed, wqkv_ref[:, :ch]) * (LOG2E * head_dim ** -0.5)).astype(BF)
    k = dot(normed, wqkv_ref[:, ch : 2 * ch]).astype(BF)
    v = dot(normed, wqkv_ref[:, 2 * ch :]).astype(BF)
    ones = jnp.ones((length, half_ch), BF)
    lane = lax.broadcasted_iota(jnp.int32, (1, ch), 1) // head_dim
    vals = [jnp.concatenate([v[:, i * half_ch : (i + 1) * half_ch], ones], 1) for i in range(2)]

    def scores(head):
        qm = jnp.where(lane == head, q, BF(0))
        return lax.dot_general(qm, k, (((1,), (1,)), ((), ())), preferred_element_type=F32)

    sums = [None, None]

    def attend(head, e):
        half = head // (HEADS // 2)
        r = dot(e, vals[half])
        parts = (r[:, :half_ch], r[:, half_ch:])
        if sums[half] is None:
            sums[half] = parts
        else:
            mine = lane[:, half * half_ch : (half + 1) * half_ch] == head
            sums[half] = tuple(jnp.where(mine, a, b) for a, b in zip(parts, sums[half]))

    s = scores(0)
    waiting = None
    for head in range(HEADS):
        e = jnp.exp2(s - jnp.max(s, -1, keepdims=True)).astype(BF)
        if head + 1 < HEADS:
            s = scores(head + 1)
        if waiting is not None:
            attend(*waiting)
        waiting = (head, e)
    attend(*waiting)
    halves = [(num * pl.reciprocal(den)).astype(BF) for num, den in sums]
    return x + dot(jnp.concatenate(halves, 1), wout_ref[...])


def split3(x):
    a = x.astype(BF).astype(F32)
    b = (x - a).astype(BF).astype(F32)
    return a, b, x - a - b


class Plan:
    def __init__(self, ny, nx, height, width):
        self.ny, self.nx = ny, nx
        self.n = ny * nx
        self.height, self.width = height, width
        self.th, self.tw = height // ny, width // nx
        self.rows = height // self.n
        self.cols = width // self.n
        self.per_group = LANES // self.tw
        self.pairs = DEPTH // self.per_group // 2

    def snake(self, q):
        return jnp.where(q < self.ny // 2, q, 3 * self.ny // 2 - 1 - q)

    def owner(self, group):
        m = lax.rem(group, 2 * self.ny)
        return (self.snake(m // 2), 2 * (group // (2 * self.ny)) + lax.rem(m, 2))


def kernel(
    pn,
    occ_ref, cnt_ref, emb_ref, cw_ref, g_ref, rqkv_ref, rout_ref, cqkv_ref, cout_ref, dk_ref, pw_ref,
    out_ref,
    snd_s, got_s, lhs_s, ee_s, x_s, s_s, r_s, xr_s, cd_s, o_s,
    all_in, occ_sems, row_send, row_recv, hsend, hrecv, out_sems,
):
    ny, nx, n = pn.ny, pn.nx, pn.n
    th, tw, rows, cols = pn.th, pn.tw, pn.rows, pn.cols
    ch = emb_ref.shape[1]
    levels = emb_ref.shape[0]
    gy, gx = lax.axis_index("gy"), lax.axis_index("gx")
    core = lax.rem(gx, 2)
    m = 2 * pn.snake(gy) + core
    group = (gx // 2) * (2 * ny) + m
    row_group = gy * nx + gx
    tile_x = 2 * (gx // 2) + m // ny
    first = lax.rem(m, ny) * cols
    has_left, has_right = group > 0, group < n - 1
    left = pn.owner(jnp.maximum(group - 1, 0))
    right = pn.owner(jnp.minimum(group + 1, n - 1))
    barrier = pltpu.get_barrier_semaphore()

    def greet(sem, along_x):
        def one(t, carry):
            other = (gy, lax.rem(gx + t, nx)) if along_x else (lax.rem(gy + t, ny), gx)
            pl.semaphore_signal(sem, inc=1, device_id=other, device_id_type=MESH)
            return carry

        lax.fori_loop(1, nx if along_x else ny, one, 0)

    greet(barrier, True)
    greet(barrier, False)

    def lined_up(b):
        logs = split3(jnp.log1p(cnt_ref[b].astype(F32)))
        terms = [logs[i] for i in (0, 0, 0, 1, 1, 2)]
        return jnp.concatenate(
            [occ_ref[b].astype(F32).reshape(levels * tw, th)]
            + terms
            + [jnp.zeros(((DEPTH - levels - len(terms)) * tw, th), F32)],
            0,
        )

    turned = jnp.concatenate([lined_up(0), lined_up(1)], 1).T
    t0 = turned[:th].reshape(th // 8, 8, DEPTH * tw)
    t1 = turned[th:].reshape(th // 8, 8, DEPTH * tw)
    sub = lax.broadcasted_iota(jnp.int32, (1, 8, 1), 1) < 4
    both = (jnp.where(sub, t0, pltpu.roll(t1, 4, 1)), jnp.where(sub, pltpu.roll(t0, 4, 1), t1))
    for t in range(th // 8):
        for i in range(2):
            for p in range(pn.pairs):
                part = both[i][t][:, 2 * p * LANES : 2 * (p + 1) * LANES]
                snd_s[2 * t + i, p] = jnp.concatenate([part[:, :LANES], part[:, LANES:]], 0).astype(BF)

    pl.semaphore_wait(barrier, nx - 1 + ny - 1)

    def send_occ(t, carry):
        to = lax.rem(gx + t, nx)
        pltpu.make_async_remote_copy(
            src_ref=snd_s.at[to],
            dst_ref=got_s.at[gx],
            send_sem=occ_sems.at[0],
            recv_sem=occ_sems.at[1],
            device_id=(gy, to),
            device_id_type=MESH,
        ).start()
        return carry

    lax.fori_loop(1, nx, send_occ, 0)
    got_s[gx] = snd_s[gx]
    greet(all_in, False)

    w1, w2, w3 = split3(cw_ref[...])
    table = [emb_ref[i : i + 1, :].astype(F32) for i in range(levels)] + [w1, w2, w3, w1, w2, w1]
    zero = jnp.zeros((8, ch), F32)
    for i in range(pn.per_group):
        for j in range(LANES // 8):
            at = j * pn.per_group + i
            r0 = i * LANES + j * 8
            ee_s[r0 : r0 + 8, :] = jnp.broadcast_to(table[at], (8, ch)) if at < len(table) else zero

    for s in range(2):
        arrived = got_s.at[pl.ds(0, nx - 1)]
        pltpu.make_async_copy(arrived, arrived, occ_sems.at[s]).wait()

    def unpack(src, carry):
        rows_in = got_s[src].reshape(pn.pairs * 16, LANES).astype(F32)
        pad = jnp.zeros((LANES - pn.pairs * 16, LANES), F32)
        back = jnp.concatenate([rows_in, pad], 0).T.astype(BF)
        for i in range(pn.per_group):
            lhs_s[pl.ds(pl.multiple_of(src * tw, tw), tw), i * LANES : (i + 1) * LANES] = back[
                i * tw : (i + 1) * tw
            ]
        return carry

    lax.fori_loop(0, nx, unpack, 0, unroll=16)
    which = lax.broadcasted_iota(jnp.int32, (pn.per_group * LANES, 1), 0) % 8

    def pillars(i, carry):
        x_s[i] = dot(lhs_s[...], jnp.where(which == i, ee_s[...], 0.0).astype(BF)).astype(BF)
        return carry

    pl.semaphore_wait(all_in, ny - 1)

    def row_sample(b, carry):
        lax.fori_loop(b * rows, (b + 1) * rows, pillars, 0)
        y = [
            section(x_s[b * rows + i].astype(F32), g_ref[0:1, :], rqkv_ref, rout_ref).reshape(n // 2, 8, ch)
            for i in range(4)
        ]
        even = [jnp.where(sub, y[i], pltpu.roll(y[i + 1], 4, 1)) for i in (0, 2)]
        odd = [jnp.where(sub, pltpu.roll(y[i], 4, 1), y[i + 1]) for i in (0, 2)]
        s_s[b, :, 0] = jnp.concatenate(even, 1).astype(BF)
        s_s[b, :, 1] = jnp.concatenate(odd, 1).astype(BF)

        def send(t):
            u = lax.rem(37 * t + gy * nx + gx, n)
            to_y, to_x = lax.div(u, nx), lax.rem(u, nx)
            q = pn.snake(to_y)
            pltpu.make_async_remote_copy(
                src_ref=s_s.at[b, lax.div(to_x, 2) * ny + q, lax.rem(to_x, 2)],
                dst_ref=r_s.at[b, row_group],
                send_sem=row_send.at[b],
                recv_sem=row_recv.at[b],
                device_id=(to_y, to_x),
                device_id_type=MESH,
            ).start()

        def send_some(t, c):
            for i in range(7):
                send(t * 7 + i + 1)
            return c

        lax.fori_loop(0, (n - 1) // 7, send_some, 0)
        for t in range((n - 1) // 7 * 7 + 1, n):
            send(t)
        r_s[b, row_group] = s_s[b, group // 2, lax.rem(group, 2)]
        return carry

    lax.fori_loop(0, 2, row_sample, 0)

    edge = jnp.zeros(cd_s.shape[2:], BF)
    for b in range(2):

        @pl.when(jnp.logical_not(has_left))
        def _():
            cd_s[b, 0] = edge

        @pl.when(jnp.logical_not(has_right))
        def _():
            cd_s[b, cols + 1] = edge

    row = lax.broadcasted_iota(jnp.int32, (pn.height, 1), 0)

    def halo(b, side):
        return pltpu.make_async_remote_copy(
            src_ref=cd_s.at[b, cols if side else 1],
            dst_ref=cd_s.at[b, 0 if side else cols + 1],
            send_sem=hsend.at[b, side],
            recv_sem=hrecv.at[b, side],
            device_id=right if side else left,
            device_id_type=MESH,
        )

    def col_sample(b, carry):
        blocks = r_s.at[b, pl.ds(0, n - 1)]
        pltpu.make_async_copy(blocks, blocks, row_recv.at[b]).wait()
        for i in range(ch // LANES):
            xr_s[i] = r_s[b, :, :, i * LANES : (i + 1) * LANES].astype(F32).reshape(pn.height * cols, LANES)

        def line(at):
            x = jnp.concatenate(
                [xr_s[j, pl.ds(at, pn.height, stride=cols), :] for j in range(ch // LANES)], 1
            )
            cd_s[b, at + 1] = section(x, g_ref[1:2, :], cqkv_ref, cout_ref).astype(BF)

        def conv(i, c):
            near = [cd_s[b, i + e].astype(F32) for e in range(3)]
            taps = [sum(near[e] * dk_ref[a, e, :][None] for e in range(3)) for a in range(3)]
            above = jnp.where(row == 0, 0.0, pltpu.roll(taps[0], 1, 0))
            below = jnp.where(row == pn.height - 1, 0.0, pltpu.roll(taps[2], pn.height - 1, 0))
            half = 0.5 * (above + taps[1] + below)
            act = (half * jnp.tanh(half) + half).astype(BF)
            o_s[b, i] = (near[1] + dot(act, pw_ref[...])).astype(BF)

            def send(t, cc):
                to = lax.rem(gy + 3 * t, ny)
                src = o_s.at[b, i, pl.ds(pl.multiple_of(to * th, th), th)]
                dst = out_ref.at[b * tw + first + i]
                away = jnp.logical_or(t > 0, tile_x != gx)

                @pl.when(away)
                def _():
                    pltpu.make_async_remote_copy(
                        src_ref=src,
                        dst_ref=dst,
                        send_sem=out_sems.at[0],
                        recv_sem=out_sems.at[1],
                        device_id=(to, tile_x),
                        device_id_type=MESH,
                    ).start()

                @pl.when(jnp.logical_not(away))
                def _():
                    pltpu.make_async_copy(src, dst, out_sems.at[2]).start()

                return cc

            lax.fori_loop(0, ny, send, 0)
            return c

        line(0)

        @pl.when(has_left)
        def _():
            halo(b, 0).start()

        line(1)
        line(2)

        def last_lines(i, c):
            @pl.when(i == 1)
            def _():
                line(3)

                @pl.when(has_right)
                def _():
                    halo(b, 1).start()

            @pl.when(jnp.logical_and(i == 2, has_right))
            def _():
                halo(b, 0).wait_recv()

            @pl.when(jnp.logical_and(i == 3, has_left))
            def _():
                halo(b, 1).wait_recv()

            conv(lax.rem(i + 1, cols), 0)
            return c

        lax.fori_loop(0, cols, last_lines, 0)
        return carry

    lax.fori_loop(0, 2, col_sample, 0)

    for b in range(2):
        blocks = r_s.at[b, pl.ds(0, n - 1)]
        pltpu.make_async_copy(blocks, blocks, row_send.at[b]).wait()

        @pl.when(has_left)
        def _():
            halo(b, 0).wait_send()

        @pl.when(has_right)
        def _():
            halo(b, 1).wait_send()

    local = tile_x == gx

    def wait_out(count, s):
        part = out_ref.at[pl.ds(0, count)]
        pltpu.make_async_copy(part, part, out_sems.at[s]).wait()

    @pl.when(local)
    def _():
        wait_out(2 * cols * (ny - 1), 0)
        wait_out(2 * cols * (ny - 1), 1)
        wait_out(2 * cols, 2)

    @pl.when(jnp.logical_not(local))
    def _():
        wait_out(2 * cols * ny, 0)
        wait_out(2 * cols * ny, 1)


def turn_kernel(parts, x_ref, o_ref, x_s, o_s, in_sems, out_sems):
    samples, _, th, _ = x_ref.shape
    step = th // parts

    def bring(b, i):
        rows = pl.ds(i * step, step)
        return pltpu.make_async_copy(x_ref.at[b, :, rows], x_s.at[b, :, rows], in_sems.at[b, i])

    def leave(b, i):
        rows = pl.ds(i * step, step)
        return pltpu.make_async_copy(o_s.at[b, rows], o_ref.at[b, rows], out_sems.at[b, i])

    order = [(b, i) for b in range(samples) for i in range(parts)]
    for at in order:
        bring(*at).start()
    for b, i in order:
        bring(b, i).wait()
        o_s[b, i * step : (i + 1) * step] = jnp.swapaxes(x_s[b, :, i * step : (i + 1) * step], 0, 1)
        leave(b, i).start()
    for at in order:
        leave(*at).wait()


def turn(x, parts):
    samples, tw, th, ch = x.shape
    return pl.pallas_call(
        functools.partial(turn_kernel, parts),
        in_specs=[pl.BlockSpec(memory_space=pl.ANY)],
        out_specs=pl.BlockSpec(memory_space=pl.ANY),
        out_shape=jax.ShapeDtypeStruct((samples, th, tw, ch), x.dtype),
        scratch_shapes=[
            pltpu.VMEM(x.shape, x.dtype),
            pltpu.VMEM((samples, th, tw, ch), x.dtype),
            pltpu.SemaphoreType.DMA((samples, parts)),
            pltpu.SemaphoreType.DMA((samples, parts)),
        ],
        compiler_params=pltpu.CompilerParams(vmem_limit_bytes=60 * 2**20),
        name="turn",
    )(x)


def per_device(
    occupancy,
    counts,
    level_embed,
    count_weight,
    norm_gains,
    row_qkv,
    row_out,
    col_qkv,
    col_out,
    depth_kernel,
    point_weight,
):
    ny, nx = lax.axis_size("gy"), lax.axis_size("gx")
    th, tw = counts.shape[1:]
    ch = level_embed.shape[1]
    pn = Plan(ny, nx, th * ny, tw * nx)
    vmem = pl.BlockSpec(memory_space=pltpu.VMEM)
    out = pl.pallas_call(
        functools.partial(kernel, pn),
        out_shape=jax.ShapeDtypeStruct((2 * tw, th, ch), BF),
        in_specs=[vmem] * 11,
        out_specs=pl.BlockSpec(memory_space=pl.ANY),
        scratch_shapes=[
            pltpu.VMEM((nx, pn.pairs, 16, LANES), BF),
            pltpu.VMEM((nx, pn.pairs, 16, LANES), BF),
            pltpu.VMEM((pn.width, pn.per_group * LANES), BF),
            pltpu.VMEM((pn.per_group * LANES, ch), F32),
            pltpu.VMEM((2 * pn.rows, pn.width, ch), BF),
            pltpu.VMEM((2, pn.n // 2, 2, 16, ch), BF),
            pltpu.VMEM((2, pn.n, 16, ch), BF),
            pltpu.VMEM((ch // LANES, pn.height * pn.cols, LANES), F32),
            pltpu.VMEM((2, pn.cols + 2, pn.height, ch), BF),
            pltpu.VMEM((2, pn.cols, pn.height, ch), BF),
            pltpu.SemaphoreType.REGULAR,
            pltpu.SemaphoreType.DMA((2,)),
            pltpu.SemaphoreType.DMA((2,)),
            pltpu.SemaphoreType.DMA((2,)),
            pltpu.SemaphoreType.DMA((2, 2)),
            pltpu.SemaphoreType.DMA((2, 2)),
            pltpu.SemaphoreType.DMA((3,)),
        ],
        compiler_params=pltpu.CompilerParams(
            collective_id=0, has_side_effects=True, vmem_limit_bytes=60 * 2**20
        ),
        name="block",
    )(
        occupancy.transpose(0, 1, 3, 2),
        counts.transpose(0, 2, 1),
        level_embed,
        count_weight[None],
        norm_gains,
        row_qkv,
        row_out,
        col_qkv,
        col_out,
        depth_kernel,
        point_weight,
    )
    return turn(out.reshape(2, tw, th, ch), 2)


def solution(mesh):
    in_specs = (P(None, None, "gy", "gx"), P(None, "gy", "gx")) + (P(),) * 9
    out_specs = P(None, "gy", "gx", None)
    return jax.shard_map(
        per_device, mesh=mesh, in_specs=in_specs, out_specs=out_specs, check_vma=False
    )
```

```python
import functools

import jax
import jax.numpy as jnp
from jax import lax
from jax.experimental import pallas as pl
from jax.experimental.pallas import tpu as pltpu
from jax.sharding import PartitionSpec as P

HEADS = 8
BF = jnp.bfloat16
F32 = jnp.float32
LOG2E = 1.4426950408889634
MESH = pl.DeviceIdType.MESH
DEPTH = 48
LANES = 128


def dot(a, b):
    return jnp.dot(a, b, preferred_element_type=F32)


def section(x, gain, wqkv_ref, wout_ref):
    length, ch = x.shape
    half_ch = ch // 2
    head_dim = ch // HEADS
    cen = x - jnp.mean(x, -1, keepdims=True)
    var = jnp.mean(cen * cen, -1, keepdims=True)
    normed = (cen * lax.rsqrt(var + 1e-5) * gain).astype(BF)
    q = (dot(normed, wqkv_ref[:, :ch]) * (LOG2E * head_dim ** -0.5)).astype(BF)
    k = dot(normed, wqkv_ref[:, ch : 2 * ch]).astype(BF)
    v = dot(normed, wqkv_ref[:, 2 * ch :]).astype(BF)
    ones = jnp.ones((length, half_ch), BF)
    lane = lax.broadcasted_iota(jnp.int32, (1, ch), 1) // head_dim
    vals = [jnp.concatenate([v[:, i * half_ch : (i + 1) * half_ch], ones], 1) for i in range(2)]

    def scores(head):
        qm = jnp.where(lane == head, q, BF(0))
        return lax.dot_general(qm, k, (((1,), (1,)), ((), ())), preferred_element_type=F32)

    sums = [None, None]

    def attend(head, e):
        half = head // (HEADS // 2)
        r = dot(e, vals[half])
        parts = (r[:, :half_ch], r[:, half_ch:])
        if sums[half] is None:
            sums[half] = parts
        else:
            mine = lane[:, half * half_ch : (half + 1) * half_ch] == head
            sums[half] = tuple(jnp.where(mine, a, b) for a, b in zip(parts, sums[half]))

    s = scores(0)
    waiting = None
    for head in range(HEADS):
        e = jnp.exp2(s - jnp.max(s, -1, keepdims=True)).astype(BF)
        if head + 1 < HEADS:
            s = scores(head + 1)
        if waiting is not None:
            attend(*waiting)
        waiting = (head, e)
    attend(*waiting)
    halves = [(num * pl.reciprocal(den)).astype(BF) for num, den in sums]
    return x + dot(jnp.concatenate(halves, 1), wout_ref[...])


def split3(x):
    a = x.astype(BF).astype(F32)
    b = (x - a).astype(BF).astype(F32)
    return a, b, x - a - b


class Plan:
    def __init__(self, ny, nx, height, width):
        self.ny, self.nx = ny, nx
        self.n = ny * nx
        self.height, self.width = height, width
        self.th, self.tw = height // ny, width // nx
        self.rows = height // self.n
        self.cols = width // self.n
        self.per_group = LANES // self.tw
        self.pairs = DEPTH // self.per_group // 2

    def snake(self, q):
        return jnp.where(q < self.ny // 2, q, 3 * self.ny // 2 - 1 - q)

    def owner(self, group):
        m = lax.rem(group, 2 * self.ny)
        return (self.snake(m // 2), 2 * (group // (2 * self.ny)) + lax.rem(m, 2))


def kernel(
    pn,
    occ_ref, cnt_ref, emb_ref, cw_ref, g_ref, rqkv_ref, rout_ref, cqkv_ref, cout_ref, dk_ref, pw_ref,
    out_ref,
    snd_s, got_s, lhs_s, ee_s, x_s, s_s, r_s, xr_s, cd_s, o_s,
    all_in, occ_sems, row_send, row_recv, hsend, hrecv, out_sems,
):
    ny, nx, n = pn.ny, pn.nx, pn.n
    th, tw, rows, cols = pn.th, pn.tw, pn.rows, pn.cols
    ch = emb_ref.shape[1]
    levels = emb_ref.shape[0]
    gy, gx = lax.axis_index("gy"), lax.axis_index("gx")
    core = lax.rem(gx, 2)
    m = 2 * pn.snake(gy) + core
    group = (gx // 2) * (2 * ny) + m
    row_group = gy * nx + gx
    tile_x = 2 * (gx // 2) + m // ny
    first = lax.rem(m, ny) * cols
    has_left, has_right = group > 0, group < n - 1
    left = pn.owner(jnp.maximum(group - 1, 0))
    right = pn.owner(jnp.minimum(group + 1, n - 1))
    barrier = pltpu.get_barrier_semaphore()

    def greet(sem, along_x):
        def one(t, carry):
            other = (gy, lax.rem(gx + t, nx)) if along_x else (lax.rem(gy + t, ny), gx)
            pl.semaphore_signal(sem, inc=1, device_id=other, device_id_type=MESH)
            return carry

        lax.fori_loop(1, nx if along_x else ny, one, 0)

    greet(barrier, True)
    greet(barrier, False)

    def lined_up(b):
        logs = split3(jnp.log1p(cnt_ref[b].astype(F32)))
        terms = [logs[i] for i in (0, 0, 0, 1, 1, 2)]
        return jnp.concatenate(
            [occ_ref[b].astype(F32).reshape(levels * tw, th)]
            + terms
            + [jnp.zeros(((DEPTH - levels - len(terms)) * tw, th), F32)],
            0,
        )

    turned = jnp.concatenate([lined_up(0), lined_up(1)], 1).T
    t0 = turned[:th].reshape(th // 8, 8, DEPTH * tw)
    t1 = turned[th:].reshape(th // 8, 8, DEPTH * tw)
    sub = lax.broadcasted_iota(jnp.int32, (1, 8, 1), 1) < 4
    both = (jnp.where(sub, t0, pltpu.roll(t1, 4, 1)), jnp.where(sub, pltpu.roll(t0, 4, 1), t1))
    for t in range(th // 8):
        for i in range(2):
            for p in range(pn.pairs):
                part = both[i][t][:, 2 * p * LANES : 2 * (p + 1) * LANES]
                snd_s[2 * t + i, p] = jnp.concatenate([part[:, :LANES], part[:, LANES:]], 0).astype(BF)

    pl.semaphore_wait(barrier, nx - 1 + ny - 1)

    def send_occ(t, carry):
        to = lax.rem(gx + t, nx)
        pltpu.make_async_remote_copy(
            src_ref=snd_s.at[to],
            dst_ref=got_s.at[gx],
            send_sem=occ_sems.at[0],
            recv_sem=occ_sems.at[1],
            device_id=(gy, to),
            device_id_type=MESH,
        ).start()
        return carry

    lax.fori_loop(1, nx, send_occ, 0, unroll=5)
    got_s[gx] = snd_s[gx]
    greet(all_in, False)

    w1, w2, w3 = split3(cw_ref[...])
    table = [emb_ref[i : i + 1, :].astype(F32) for i in range(levels)] + [w1, w2, w3, w1, w2, w1]
    zero = jnp.zeros((8, ch), F32)
    for i in range(pn.per_group):
        for j in range(LANES // 8):
            at = j * pn.per_group + i
            r0 = i * LANES + j * 8
            ee_s[r0 : r0 + 8, :] = jnp.broadcast_to(table[at], (8, ch)) if at < len(table) else zero

    for s in range(2):
        arrived = got_s.at[pl.ds(0, nx - 1)]
        pltpu.make_async_copy(arrived, arrived, occ_sems.at[s]).wait()

    def unpack(src, carry):
        rows_in = got_s[src].reshape(pn.pairs * 16, LANES).astype(F32)
        pad = jnp.zeros((LANES - pn.pairs * 16, LANES), F32)
        back = jnp.concatenate([rows_in, pad], 0).T.astype(BF)
        for i in range(pn.per_group):
            lhs_s[pl.ds(pl.multiple_of(src * tw, tw), tw), i * LANES : (i + 1) * LANES] = back[
                i * tw : (i + 1) * tw
            ]
        return carry

    lax.fori_loop(0, nx, unpack, 0, unroll=16)
    which = lax.broadcasted_iota(jnp.int32, (pn.per_group * LANES, 1), 0) % 8

    def pillars(i, carry):
        x_s[i] = dot(lhs_s[...], jnp.where(which == i, ee_s[...], 0.0).astype(BF)).astype(BF)
        return carry

    pl.semaphore_wait(all_in, ny - 1)

    def row_sample(b, carry):
        lax.fori_loop(b * rows, (b + 1) * rows, pillars, 0)
        y = [
            section(x_s[b * rows + i].astype(F32), g_ref[0:1, :], rqkv_ref, rout_ref).reshape(n // 2, 8, ch)
            for i in range(4)
        ]
        even = [jnp.where(sub, y[i], pltpu.roll(y[i + 1], 4, 1)) for i in (0, 2)]
        odd = [jnp.where(sub, pltpu.roll(y[i], 4, 1), y[i + 1]) for i in (0, 2)]
        s_s[b, :, 0] = jnp.concatenate(even, 1).astype(BF)
        s_s[b, :, 1] = jnp.concatenate(odd, 1).astype(BF)

        def send(t):
            u = lax.rem(37 * t + gy * nx + gx, n)
            to_y, to_x = lax.div(u, nx), lax.rem(u, nx)
            q = pn.snake(to_y)
            pltpu.make_async_remote_copy(
                src_ref=s_s.at[b, lax.div(to_x, 2) * ny + q, lax.rem(to_x, 2)],
                dst_ref=r_s.at[b, row_group],
                send_sem=row_send.at[b],
                recv_sem=row_recv.at[b],
                device_id=(to_y, to_x),
                device_id_type=MESH,
            ).start()

        def send_some(t, c):
            for i in range(7):
                send(t * 7 + i + 1)
            return c

        lax.fori_loop(0, (n - 1) // 7, send_some, 0)
        for t in range((n - 1) // 7 * 7 + 1, n):
            send(t)
        r_s[b, row_group] = s_s[b, group // 2, lax.rem(group, 2)]
        return carry

    lax.fori_loop(0, 2, row_sample, 0)

    edge = jnp.zeros(cd_s.shape[2:], BF)
    for b in range(2):

        @pl.when(jnp.logical_not(has_left))
        def _():
            cd_s[b, 0] = edge

        @pl.when(jnp.logical_not(has_right))
        def _():
            cd_s[b, cols + 1] = edge

    row = lax.broadcasted_iota(jnp.int32, (pn.height, 1), 0)

    def halo(b, side):
        return pltpu.make_async_remote_copy(
            src_ref=cd_s.at[b, cols if side else 1],
            dst_ref=cd_s.at[b, 0 if side else cols + 1],
            send_sem=hsend.at[b, side],
            recv_sem=hrecv.at[b, side],
            device_id=right if side else left,
            device_id_type=MESH,
        )

    def col_sample(b, carry):
        blocks = r_s.at[b, pl.ds(0, n - 1)]
        pltpu.make_async_copy(blocks, blocks, row_recv.at[b]).wait()
        for i in range(ch // LANES):
            xr_s[i] = r_s[b, :, :, i * LANES : (i + 1) * LANES].astype(F32).reshape(pn.height * cols, LANES)

        def line(at):
            x = jnp.concatenate(
                [xr_s[j, pl.ds(at, pn.height, stride=cols), :] for j in range(ch // LANES)], 1
            )
            cd_s[b, at + 1] = section(x, g_ref[1:2, :], cqkv_ref, cout_ref).astype(BF)

        def conv(i, c):
            near = [cd_s[b, i + e].astype(F32) for e in range(3)]
            taps = [sum(near[e] * dk_ref[a, e, :][None] for e in range(3)) for a in range(3)]
            above = jnp.where(row == 0, 0.0, pltpu.roll(taps[0], 1, 0))
            below = jnp.where(row == pn.height - 1, 0.0, pltpu.roll(taps[2], pn.height - 1, 0))
            half = 0.5 * (above + taps[1] + below)
            act = (half * jnp.tanh(half) + half).astype(BF)
            o_s[b, i] = (near[1] + dot(act, pw_ref[...])).astype(BF)

            def send(t, cc):
                to = lax.rem(gy + 3 * t, ny)
                src = o_s.at[b, i, pl.ds(pl.multiple_of(to * th, th), th)]
                dst = out_ref.at[b * tw + first + i]
                away = jnp.logical_or(t > 0, tile_x != gx)

                @pl.when(away)
                def _():
                    pltpu.make_async_remote_copy(
                        src_ref=src,
                        dst_ref=dst,
                        send_sem=out_sems.at[0],
                        recv_sem=out_sems.at[1],
                        device_id=(to, tile_x),
                        device_id_type=MESH,
                    ).start()

                @pl.when(jnp.logical_not(away))
                def _():
                    pltpu.make_async_copy(src, dst, out_sems.at[2]).start()

                return cc

            lax.fori_loop(0, ny, send, 0)
            return c

        line(0)

        @pl.when(has_left)
        def _():
            halo(b, 0).start()

        line(1)
        line(2)

        def last_lines(i, c):
            @pl.when(i == 1)
            def _():
                line(3)

                @pl.when(has_right)
                def _():
                    halo(b, 1).start()

            @pl.when(jnp.logical_and(i == 2, has_right))
            def _():
                halo(b, 0).wait_recv()

            @pl.when(jnp.logical_and(i == 3, has_left))
            def _():
                halo(b, 1).wait_recv()

            conv(lax.rem(i + 1, cols), 0)
            return c

        lax.fori_loop(0, cols, last_lines, 0)
        return carry

    lax.fori_loop(0, 2, col_sample, 0)

    for b in range(2):
        blocks = r_s.at[b, pl.ds(0, n - 1)]
        pltpu.make_async_copy(blocks, blocks, row_send.at[b]).wait()

        @pl.when(has_left)
        def _():
            halo(b, 0).wait_send()

        @pl.when(has_right)
        def _():
            halo(b, 1).wait_send()

    local = tile_x == gx

    def wait_out(count, s):
        part = out_ref.at[pl.ds(0, count)]
        pltpu.make_async_copy(part, part, out_sems.at[s]).wait()

    @pl.when(local)
    def _():
        wait_out(2 * cols * (ny - 1), 0)
        wait_out(2 * cols * (ny - 1), 1)
        wait_out(2 * cols, 2)

    @pl.when(jnp.logical_not(local))
    def _():
        wait_out(2 * cols * ny, 0)
        wait_out(2 * cols * ny, 1)


def turn_kernel(parts, x_ref, o_ref, x_s, o_s, in_sems, out_sems):
    samples, _, th, _ = x_ref.shape
    step = th // parts

    def bring(b, i):
        rows = pl.ds(i * step, step)
        return pltpu.make_async_copy(x_ref.at[b, :, rows], x_s.at[b, :, rows], in_sems.at[b, i])

    def leave(b, i):
        rows = pl.ds(i * step, step)
        return pltpu.make_async_copy(o_s.at[b, rows], o_ref.at[b, rows], out_sems.at[b, i])

    order = [(b, i) for b in range(samples) for i in range(parts)]
    for at in order:
        bring(*at).start()
    for b, i in order:
        bring(b, i).wait()
        o_s[b, i * step : (i + 1) * step] = jnp.swapaxes(x_s[b, :, i * step : (i + 1) * step], 0, 1)
        leave(b, i).start()
    for at in order:
        leave(*at).wait()


def turn(x, parts):
    samples, tw, th, ch = x.shape
    return pl.pallas_call(
        functools.partial(turn_kernel, parts),
        in_specs=[pl.BlockSpec(memory_space=pl.ANY)],
        out_specs=pl.BlockSpec(memory_space=pl.ANY),
        out_shape=jax.ShapeDtypeStruct((samples, th, tw, ch), x.dtype),
        scratch_shapes=[
            pltpu.VMEM(x.shape, x.dtype),
            pltpu.VMEM((samples, th, tw, ch), x.dtype),
            pltpu.SemaphoreType.DMA((samples, parts)),
            pltpu.SemaphoreType.DMA((samples, parts)),
        ],
        compiler_params=pltpu.CompilerParams(vmem_limit_bytes=60 * 2**20),
        name="turn",
    )(x)


def per_device(
    occupancy,
    counts,
    level_embed,
    count_weight,
    norm_gains,
    row_qkv,
    row_out,
    col_qkv,
    col_out,
    depth_kernel,
    point_weight,
):
    ny, nx = lax.axis_size("gy"), lax.axis_size("gx")
    th, tw = counts.shape[1:]
    ch = level_embed.shape[1]
    pn = Plan(ny, nx, th * ny, tw * nx)
    vmem = pl.BlockSpec(memory_space=pltpu.VMEM)
    out = pl.pallas_call(
        functools.partial(kernel, pn),
        out_shape=jax.ShapeDtypeStruct((2 * tw, th, ch), BF),
        in_specs=[vmem] * 11,
        out_specs=pl.BlockSpec(memory_space=pl.ANY),
        scratch_shapes=[
            pltpu.VMEM((nx, pn.pairs, 16, LANES), BF),
            pltpu.VMEM((nx, pn.pairs, 16, LANES), BF),
            pltpu.VMEM((pn.width, pn.per_group * LANES), BF),
            pltpu.VMEM((pn.per_group * LANES, ch), F32),
            pltpu.VMEM((2 * pn.rows, pn.width, ch), BF),
            pltpu.VMEM((2, pn.n // 2, 2, 16, ch), BF),
            pltpu.VMEM((2, pn.n, 16, ch), BF),
            pltpu.VMEM((ch // LANES, pn.height * pn.cols, LANES), F32),
            pltpu.VMEM((2, pn.cols + 2, pn.height, ch), BF),
            pltpu.VMEM((2, pn.cols, pn.height, ch), BF),
            pltpu.SemaphoreType.REGULAR,
            pltpu.SemaphoreType.DMA((2,)),
            pltpu.SemaphoreType.DMA((2,)),
            pltpu.SemaphoreType.DMA((2,)),
            pltpu.SemaphoreType.DMA((2, 2)),
            pltpu.SemaphoreType.DMA((2, 2)),
            pltpu.SemaphoreType.DMA((3,)),
        ],
        compiler_params=pltpu.CompilerParams(
            collective_id=0, has_side_effects=True, vmem_limit_bytes=60 * 2**20
        ),
        name="block",
    )(
        occupancy.transpose(0, 1, 3, 2),
        counts.transpose(0, 2, 1),
        level_embed,
        count_weight[None],
        norm_gains,
        row_qkv,
        row_out,
        col_qkv,
        col_out,
        depth_kernel,
        point_weight,
    )
    return turn(out.reshape(2, tw, th, ch), 4)


def solution(mesh):
    in_specs = (P(None, None, "gy", "gx"), P(None, "gy", "gx")) + (P(),) * 9
    out_specs = P(None, "gy", "gx", None)
    return jax.shard_map(
        per_device, mesh=mesh, in_specs=in_specs, out_specs=out_specs, check_vma=False
    )
```
